32 devices in a mesh: grp: 2 (over x), seq: 16 (over z, y, core).
Axes of the slice: x: 2, y: 2, z: 4, core: 2. Of those that a mesh axis runs over, the one named last changes fastest.
Arguments:
- projected: bfloat16 [8192, 3, 1024], P(('grp', 'seq')), parts along dimension 0, may hold values from -6 to 6
- taps: float32 [3, 3, 1024], replicated, may hold values from -3.5 to 3.5
- filters: bfloat16 [1024, 4096], P('seq'), may hold values from -0.09375 to 0.09375
- skip: float32 [1024], P('seq'), may hold values from 0.5 to 1.5
Outputs:
- output: bfloat16 [8192, 1024], P(('grp', 'seq')), parts along dimension 0
The draws below stay inside these ranges and needn't reach their ends.
There are 2 independent parts, one for each index of `grp`. The reference program is written for one: setup_inputs(seed, part) draws one part's arguments, and reference() takes and returns one part's arrays. A program takes and returns all parts, laid end to end along the dimension named above; an argument that names none is the same for every part. Nothing has to cross between parts.
All inputs are finite; a program needn't handle non-finite values.
Results may differ from the reference program's by a relative error of at most 0.009.
Values may be sent and summed in bfloat16 or wider, within the bound.
A program may use at most 64 MiB of HBM per device.

```python
import jax
import jax.numpy as jnp
from jax import lax

C = 1024
SHORT = 3
L = 4096


def level_of(key, extent, cuts, low, top_value):
    level, own = 1.0, jax.random.fold_in(key, 6)
    for dim, parts in cuts:
        steps = jnp.exp(jax.random.uniform(jax.random.fold_in(own, dim), (parts,), jnp.float32, low / len(cuts), top_value / len(cuts)))
        level = level * jnp.repeat(steps, extent[dim] // parts).reshape([-1 if axis == dim else 1 for axis in range(len(extent))])
    return level


def normal_values(key, extent, deviation, reach, split=(), dtype=jnp.bfloat16):
    entries = jax.random.normal(key, extent, jnp.float32) * deviation
    if len(split) > 0:
        entries = level_of(key, extent, split, -0.22, 0.18) * entries
    return jnp.clip(entries, min=-reach, max=reach).astype(dtype)


def setup_inputs(seed: int = 0, part: int = 0) -> dict:
    seeds = jax.random.split(jax.random.key(seed), 5)
    part_splits = jax.random.split(jax.random.fold_in(seeds[4], part), 5)
    return {
        "projected": normal_values(part_splits[0], (L, 3, C), 1.0, 6.0, ((0, 16),)),
        "taps": normal_values(seeds[1], (SHORT, 3, C), SHORT ** -0.5, 3.5, (), jnp.float32),
        "filters": normal_values(seeds[2], (C, L), L ** -0.5, 0.09375, ((0, 16),)),
        "skip": jnp.clip(0.5 + 1.0 * jax.random.uniform(seeds[3], (C,), jnp.float32) ** level_of(seeds[3], (C,), ((0, 16),), -0.2, 0.2), 0.5, 1.5),
    }


def reference(projected, taps, filters, skip):
    length = projected.shape[0]
    source = projected.astype(jnp.float32)
    features = jnp.zeros(source.shape, jnp.float32)
    for offset in range(SHORT):
        moved = jnp.pad(source, ((offset, 0), (0, 0), (0, 0)))[:length]
        features = features + taps[offset].astype(jnp.float32) * moved
    drive = (features[:, 1] * features[:, 2]).astype(jnp.bfloat16)
    signal = drive.astype(jnp.float32).T
    kernel = filters.astype(jnp.float32)
    channels = signal.shape[0]

    def convolve(pair):
        first, second = pair
        spectrum = jnp.fft.rfft(first, 2 * length, axis=-1) * jnp.fft.rfft(second, 2 * length, axis=-1)
        return jnp.fft.irfft(spectrum, 2 * length, axis=-1)[:, :length].astype(jnp.float32)

    blocks = channels // 64
    conv = lax.map(convolve, (signal.reshape(blocks, 64, length), kernel.reshape(blocks, 64, length)))
    conv = conv.reshape(channels, length)
    long = (conv + skip.astype(jnp.float32)[:, None] * signal).astype(jnp.bfloat16)
    return (features[:, 0] * long.T.astype(jnp.float32)).astype(jnp.bfloat16)
```

```python
import functools
import math

import jax
import jax.numpy as jnp
import numpy as np
from jax import lax
from jax.experimental import pallas as pl
from jax.experimental.pallas import tpu as pltpu
from jax.sharding import PartitionSpec as P

LANES = 128
SUB = 8
F32 = jnp.float32
BF16 = jnp.bfloat16


def factors(order):
    inner = 1 << (int(math.log2(order)) // 2)
    return order // inner, inner


def dft_tables(order):
    n1, n2 = factors(order)
    half, hb = n1 // 2, n2 // 2
    groups = n2 // SUB
    s = np.arange(half)[:, None, None]
    a = np.arange(half)[None, :, None]
    b = np.arange(n2)[None, None, :]
    theta = 2 * np.pi * ((s * (a * n2 + b)) % order) / order
    sign = np.broadcast_to((-1.0) ** np.arange(half)[:, None], (half, n2))
    fwd = np.stack((np.cos(theta), -np.sin(theta)), 1)
    fwd[0, 0] = 1.0
    fwd[0, 1] = sign
    inv = np.stack((2 * np.cos(theta), -2 * np.sin(theta)), 1)
    inv[0, 0] = 1.0
    inv[0, 1] = sign
    inv = inv / order
    eye = np.eye(SUB)
    fwd_g = fwd.reshape(half, 2, half, groups, SUB)
    first = np.einsum("srage,ef->gsreaf", fwd_g, eye).reshape(groups, 2 * half * SUB, half * SUB)
    inv_g = inv.reshape(half, 2, half, groups, SUB)
    last = np.einsum("srage,ef->gaesrf", inv_g, eye).reshape(groups, half * SUB, 2 * half * SUB)
    k = np.arange(n2)
    phi = 2 * np.pi * (np.outer(k, k) % n2) / n2
    c, d = np.cos(phi), np.sin(phi)
    mid = np.block([[c, d], [-d, c]])
    back = np.block([[c, -d], [d, c]])
    kh = np.arange(hb)
    low = 2 * np.pi * (np.outer(kh, k) % n2) / n2
    odd = 2 * np.pi * (np.outer(half + n1 * kh, k) % order) / order
    mid0 = np.zeros((2 * n2, 2 * n2))
    mid0[:hb, :n2] = np.cos(low)
    mid0[hb:n2, n2:] = np.cos(odd)
    mid0[n2 : n2 + hb, :n2] = -np.sin(low)
    mid0[n2, :n2] = (-1.0) ** k
    mid0[n2 + hb :, n2:] = -np.sin(odd)
    back0 = 2 * mid0.T
    back0[:, 0] /= 2
    back0[:, n2] /= 2
    cast = lambda x: x.astype(BF16)
    return cast(first), cast(np.stack((mid0, mid))), cast(np.stack((back0, back))), cast(last)


def kernel(
    n,
    proj, taps, filt, skip, first, mid, back, last,
    out,
    margin, query, drive, pack, recv, sig, tok, spec_f, spec, done, ret,
    m_send, m_recv, send1, recv1, send2, recv2,
):
    me = lax.axis_index("seq")
    rows = proj.shape[0]
    chans = proj.shape[1] // 3
    count = taps.shape[0]
    lc = chans // n
    p = LANES // lc
    rpd = rows // p
    total = rpd * n
    n1, n2 = factors(2 * total)
    half = n1 // 2
    groups = n2 // SUB
    tiles = chans // LANES
    mrows = margin.shape[0]
    lane = lax.broadcasted_iota(jnp.int32, (1, LANES), 1) // lc

    barrier = pltpu.get_barrier_semaphore()

    @pl.loop(1, n)
    def _(i):
        pl.semaphore_signal(barrier, inc=1, device_id={"seq": lax.rem(me + i, n)})

    pl.semaphore_wait(barrier, n - 1)

    m_copy = pltpu.make_async_remote_copy(
        src_ref=proj.at[pl.ds(rows - mrows, mrows)],
        dst_ref=margin,
        send_sem=m_send,
        recv_sem=m_recv,
        device_id={"seq": lax.rem(me + 1, n)},
    )

    @pl.when(me < n - 1)
    def _():
        m_copy.start()

    @pl.when(me > 0)
    def _():
        m_copy.wait_recv()

    @pl.when(me == 0)
    def _():
        margin[...] = jnp.zeros_like(margin)

    def exchange(i, src, dst, ssem, rsem):
        return pltpu.make_async_remote_copy(
            src_ref=src.at[lax.rem(me + i, n)],
            dst_ref=dst.at[me],
            send_sem=ssem.at[i],
            recv_sem=rsem.at[i],
            device_id={"seq": lax.rem(me + i, n)},
        )

    @pl.loop(0, tiles)
    def _(step):
        tile = lax.rem(me // p + tiles // 2 + step, tiles)
        feats = []
        for m in range(3):
            cols = pl.ds(pl.multiple_of(m * chans + tile * LANES, LANES), LANES)
            ext = jnp.concatenate((margin[:, cols], proj[:, cols]), 0).astype(F32)
            acc = None
            for o in range(count):
                tap = taps[o, m : m + 1, pl.ds(pl.multiple_of(tile * LANES, LANES), LANES)]
                term = tap * ext[mrows - o : mrows - o + rows]
                acc = term if acc is None else acc + term
            feats.append(acc)
        query[tile] = feats[0]
        drive[...] = (feats[1] * feats[2]).astype(BF16).astype(F32)
        parts = [drive[pl.ds(h, rpd, stride=p), :] for h in range(p)]
        for d in range(p):
            block = parts[d] if d == 0 else None
            block = None
            for h in range(p):
                shift = ((h - d) % p) * lc
                moved = parts[h] if shift == 0 else pltpu.roll(parts[h], shift, 1)
                block = moved if block is None else jnp.where(lane == h, moved, block)
            block = block.astype(BF16)
            dest = tile * p + d

            @pl.when(dest == me)
            def _():
                recv[me] = block

            @pl.when(dest != me)
            def _():
                pack[dest] = block
                exchange(lax.rem(dest - me + n, n), pack, recv, send1, recv1).start()

    span = LANES
    tok[0:SUB, :] = jnp.zeros((SUB, LANES), F32)

    @pl.loop(0, total * p // span)
    def _(t):
        block = filt[:, pl.ds(pl.multiple_of(t * span, span), span)].astype(F32)
        block = jnp.concatenate([block] * p, 0)
        tok[pl.ds(pl.multiple_of(SUB + t * span, SUB), span), :] = block.T

    @pl.loop(0, groups)
    def _(g):
        wide = []
        for b in range(p):
            col = []
            for a in range(half):
                at = SUB + b + p * (a * n2 + SUB * g)
                now = tok[pl.ds(at, SUB, stride=p), :]
                if b > 0:
                    old = tok[pl.ds(at - p, SUB, stride=p), :]
                    now = jnp.where(lane < b, old, now)
                col.append(now)
            wide.append(jnp.concatenate(col, 0).astype(BF16))
        wide = jnp.concatenate(wide, 1)
        res = jnp.dot(first[g], wide, preferred_element_type=F32)
        spec_f[:, :, pl.ds(pl.multiple_of(SUB * g, SUB), SUB), :] = res.reshape(half, 2, SUB, p * LANES)

    @pl.loop(0, half)
    def _(s):
        x = spec_f[s].reshape(2 * n2, p * LANES).astype(BF16)
        z = jnp.dot(mid[jnp.minimum(s, 1)], x, preferred_element_type=F32)
        spec_f[s] = z.reshape(2, n2, p * LANES)

    @pl.when(me < n - 1)
    def _():
        m_copy.wait_send()

    @pl.loop(1, n)
    def _(i):
        exchange(i, pack, recv, send1, recv1).wait()

    @pl.loop(0, n)
    def _(j):
        sig[pl.ds(pl.multiple_of(j * rpd, SUB), rpd), :] = recv[j].astype(F32)

    @pl.loop(0, groups)
    def _(g):
        x = jnp.concatenate(
            [sig[pl.ds(pl.multiple_of(a * n2 + SUB * g, SUB), SUB), :] for a in range(half)], 0
        ).astype(BF16)
        res = jnp.dot(first[g], x, preferred_element_type=F32)
        spec[:, :, pl.ds(pl.multiple_of(SUB * g, SUB), SUB), :] = res.reshape(half, 2, SUB, LANES)

    def slab(s, which, special):
        x = spec[s].reshape(2 * n2, LANES).astype(BF16)
        z = jnp.dot(mid[which], x, preferred_element_type=F32)
        zr, zi = z[:n2], z[n2:]
        rr = ii = cross = None
        for b in range(p):
            xr = zr if b == 0 else pltpu.roll(zr, b * lc, 1)
            xi = zi if b == 0 else pltpu.roll(zi, b * lc, 1)
            gr = spec_f[s, 0, :, b * LANES : (b + 1) * LANES]
            gi = spec_f[s, 1, :, b * LANES : (b + 1) * LANES]
            add = lambda t, v: v if t is None else t + v
            rr = add(rr, xr * gr)
            ii = add(ii, xi * gi)
            cross = add(cross, xr * gi + xi * gr)
        if special:
            top = lax.broadcasted_iota(jnp.int32, (n2, LANES), 0) == 0
            yr = jnp.where(top, rr, rr - ii)
            yi = jnp.where(top, ii, cross)
        else:
            yr, yi = rr - ii, cross
        y = jnp.concatenate((yr, yi), 0).astype(BF16)
        v = jnp.dot(back[which], y, preferred_element_type=F32)
        spec[s] = v.reshape(2, n2, LANES)

    slab(0, 0, True)

    @pl.loop(1, half)
    def _(s):
        slab(s, 1, False)

    direct = jnp.concatenate([skip[...]] * p, 1)

    @pl.loop(0, groups)
    def _(g):
        v = spec[:, :, pl.ds(pl.multiple_of(SUB * g, SUB), SUB), :]
        v = v.reshape(2 * half * SUB, LANES).astype(BF16)
        y = jnp.dot(last[g], v, preferred_element_type=F32)
        for a in range(half):
            at = pl.ds(pl.multiple_of(a * n2 + SUB * g, SUB), SUB)
            sig[at, :] = y[a * SUB : (a + 1) * SUB] + direct * sig[at, :]

    @pl.loop(0, n)
    def _(j):
        block = sig[pl.ds(pl.multiple_of(j * rpd, SUB), rpd), :].astype(BF16)

        @pl.when(j == me)
        def _():
            ret[me] = block

        @pl.when(j != me)
        def _():
            done[j] = block

    @pl.loop(1, n)
    def _(i):
        exchange(i, done, ret, send2, recv2).start()

    @pl.loop(1, n)
    def _(i):
        exchange(i, done, ret, send2, recv2).wait()

    @pl.loop(0, tiles)
    def _(tile):
        parts = [ret[tile * p + d].astype(F32) for d in range(p)]
        for h in range(p):
            block = None
            for d in range(p):
                shift = ((d - h) % p) * lc
                moved = parts[d] if shift == 0 else pltpu.roll(parts[d], shift, 1)
                block = moved if block is None else jnp.where(lane == d, moved, block)
            drive[pl.ds(h, rpd, stride=p), :] = block
        res = (query[tile] * drive[...]).astype(BF16)
        out[:, pl.ds(pl.multiple_of(tile * LANES, LANES), LANES)] = res


def body(n, projected, taps, filters, skip):
    rows, _, chans = projected.shape
    lc, length = filters.shape
    p = LANES // lc
    rpd = rows // p
    total = length // p
    n1, n2 = factors(2 * total)
    half = n1 // 2
    tables = dft_tables(2 * total)
    vmem = pl.BlockSpec(memory_space=pltpu.VMEM)
    return pl.pallas_call(
        functools.partial(kernel, n),
        out_shape=jax.ShapeDtypeStruct((rows, chans), BF16),
        in_specs=[vmem] * 8,
        out_specs=vmem,
        scratch_shapes=[
            pltpu.VMEM((16, 3 * chans), BF16),
            pltpu.VMEM((chans // LANES, rows, LANES), F32),
            pltpu.VMEM((rows, LANES), F32),
            pltpu.VMEM((n, rpd, LANES), BF16),
            pltpu.VMEM((n, rpd, LANES), BF16),
            pltpu.VMEM((total, LANES), F32),
            pltpu.VMEM((SUB + length, LANES), F32),
            pltpu.VMEM((half, 2, n2, p * LANES), F32),
            pltpu.VMEM((half, 2, n2, LANES), F32),
            pltpu.VMEM((n, rpd, LANES), BF16),
            pltpu.VMEM((n, rpd, LANES), BF16),
            pltpu.SemaphoreType.DMA,
            pltpu.SemaphoreType.DMA,
            pltpu.SemaphoreType.DMA((n,)),
            pltpu.SemaphoreType.DMA((n,)),
            pltpu.SemaphoreType.DMA((n,)),
            pltpu.SemaphoreType.DMA((n,)),
        ],
        compiler_params=pltpu.CompilerParams(
            collective_id=0, has_side_effects=True, vmem_limit_bytes=56 * 1024 * 1024
        ),
    )(
        projected.reshape(rows, 3 * chans), taps, filters, skip.reshape(1, lc),
        *[jnp.asarray(t) for t in tables],
    )


def solution(mesh):
    placed = (P(("grp", "seq"), None, None), P(), P("seq", None), P("seq"))
    return jax.shard_map(
        functools.partial(body, mesh.shape["seq"]),
        mesh=mesh, in_specs=placed, out_specs=P(("grp", "seq"), None), check_vma=False,
    )
```

```python
import functools
import math

import jax
import jax.numpy as jnp
import numpy as np
from jax import lax
from jax.experimental import pallas as pl
from jax.experimental.pallas import tpu as pltpu
from jax.sharding import PartitionSpec as P

LANES = 128
SUB = 8
MAX_PHASES = 4
F32 = jnp.float32
BF16 = jnp.bfloat16


def factors(order):
    inner = 1 << ((int(math.log2(order)) + 1) // 2)
    return order // inner, inner


def dft_tables(order):
    n1, n2 = factors(order)
    half, hb = n1 // 2, n2 // 2
    groups = n2 // SUB
    s = np.arange(half)[:, None, None]
    a = np.arange(half)[None, :, None]
    b = np.arange(n2)[None, None, :]
    theta = 2 * np.pi * ((s * (a * n2 + b)) % order) / order
    sign = np.broadcast_to((-1.0) ** np.arange(half)[:, None], (half, n2))
    fwd = np.stack((np.cos(theta), -np.sin(theta)), 1)
    fwd[0, 0] = 1.0
    fwd[0, 1] = sign
    inv = np.stack((2 * np.cos(theta), -2 * np.sin(theta)), 1)
    inv[0, 0] = 1.0
    inv[0, 1] = sign
    inv = inv / order
    eye = np.eye(SUB)
    fwd_g = fwd.reshape(half, 2, half, groups, SUB)
    first = np.einsum("srage,ef->gsreaf", fwd_g, eye).reshape(groups, 2 * half * SUB, half * SUB)
    inv_g = inv.reshape(half, 2, half, groups, SUB)
    last = np.einsum("srage,ef->gaesrf", inv_g, eye).reshape(groups, half * SUB, 2 * half * SUB)
    k = np.arange(n2)
    phi = 2 * np.pi * (np.outer(k, k) % n2) / n2
    c, d = np.cos(phi), np.sin(phi)
    mid = np.block([[c, d], [-d, c]])
    back = np.block([[c, -d], [d, c]])
    kh = np.arange(hb)
    low = 2 * np.pi * (np.outer(kh, k) % n2) / n2
    odd = 2 * np.pi * (np.outer(half + n1 * kh, k) % order) / order
    mid0 = np.zeros((2 * n2, 2 * n2))
    mid0[:hb, :n2] = np.cos(low)
    mid0[hb:n2, n2:] = np.cos(odd)
    mid0[n2 : n2 + hb, :n2] = -np.sin(low)
    mid0[n2, :n2] = (-1.0) ** k
    mid0[n2 + hb :, n2:] = -np.sin(odd)
    back0 = 2 * mid0.T
    back0[:, 0] /= 2
    back0[:, n2] /= 2
    cast = lambda x: np.ascontiguousarray(x.astype(BF16))
    return cast(first), cast(np.stack((mid0, mid))), cast(np.stack((back0, back))), cast(last)


def plan(chans, lc, n):
    chunks = max(1, MAX_PHASES * lc // LANES)
    lc = lc // chunks
    return chunks, lc, LANES // lc


def kernel(
    n, chunks,
    proj_hbm, taps, filt_hbm, skip, first_hbm, mid_hbm, back_hbm, last_hbm,
    out,
    proj, filt, first, mid, back, last,
    margin, query, drive, pack, recv, sig, tok, spec_f, spec, done, ret,
    load, m_send, m_recv, send1, recv1, send2, recv2,
):
    me = lax.axis_index("seq")
    _, rows, chans = proj.shape
    count = taps.shape[0]
    lc = chans // n // chunks
    p = LANES // lc
    rpd = rows // p
    total = rpd * n
    n1, n2 = factors(2 * total)
    half = n1 // 2
    groups = n2 // SUB
    tiles = chans // LANES
    own = p // chunks
    mrows = margin.shape[1]
    lead = tok.shape[1] - filt.shape[1]
    lane = lax.broadcasted_iota(jnp.int32, (1, LANES), 1) // lc

    loads = [
        pltpu.make_async_copy(a, b, load.at[k])
        for k, (a, b) in enumerate(
            ((proj_hbm, proj), (filt_hbm, filt), (first_hbm, first), (mid_hbm, mid), (back_hbm, back), (last_hbm, last))
        )
    ]
    for c in loads:
        c.start()

    barrier = pltpu.get_barrier_semaphore()

    @pl.loop(1, n)
    def _(i):
        pl.semaphore_signal(barrier, inc=1, device_id={"seq": lax.rem(me + i, n)})

    def lanes_of(tile):
        return pl.ds(pl.multiple_of(tile * LANES, LANES), LANES)

    def features(tile, ext, many):
        feats = []
        for m in range(3):
            x = ext(m)
            from_row = x.shape[0] - many
            acc = None
            for o in range(count):
                term = taps[o, m : m + 1, lanes_of(tile)] * x[from_row - o : from_row - o + many]
                acc = term if acc is None else acc + term
            feats.append(acc)
        return feats[0], (feats[1] * feats[2]).astype(BF16).astype(F32)

    def tile_features(tile):
        zero = jnp.zeros((SUB, LANES), F32)
        q, d = features(
            tile, lambda m: jnp.concatenate((zero, proj[m, :, lanes_of(tile)].astype(F32)), 0), rows
        )
        query[tile] = q
        drive[tile] = d

    loads[0].wait()
    pl.loop(0, tiles // 2)(tile_features)

    pl.semaphore_wait(barrier, n - 1)
    m_copy = pltpu.make_async_remote_copy(
        src_ref=proj.at[:, pl.ds(rows - mrows, mrows)],
        dst_ref=margin,
        send_sem=m_send,
        recv_sem=m_recv,
        device_id={"seq": lax.rem(me + 1, n)},
    )

    @pl.when(me < n - 1)
    def _():
        m_copy.start()

    pl.loop(tiles // 2, tiles)(tile_features)

    @pl.when(me > 0)
    def _():
        m_copy.wait_recv()

    @pl.when(me == 0)
    def _():
        margin[...] = jnp.zeros_like(margin)

    def exchange(k, i, src, dst, ssem, rsem):
        return pltpu.make_async_remote_copy(
            src_ref=src.at[k, lax.rem(me + i, n)],
            dst_ref=dst.at[k, me],
            send_sem=ssem.at[k, i],
            recv_sem=rsem.at[k, i],
            device_id={"seq": lax.rem(me + i, n)},
        )

    @pl.loop(0, tiles)
    def _(step):
        tile = lax.rem(me // own + tiles // 2 + step, tiles)

        def ext(m):
            before = margin[m, :, lanes_of(tile)].astype(F32)
            after = proj[m, 0:16, lanes_of(tile)].astype(F32)
            return jnp.concatenate((before[mrows - SUB :], after[:SUB]), 0)

        q, dr = features(tile, ext, SUB)
        query[tile, 0:SUB] = q
        drive[tile, 0:SUB] = dr
        parts = [drive[tile, pl.ds(h, rpd, stride=p), :] for h in range(p)]
        for d in range(p):
            block = None
            for h in range(p):
                shift = ((h - d) % p) * lc
                moved = parts[h] if shift == 0 else pltpu.roll(parts[h], shift, 1)
                block = moved if block is None else jnp.where(lane == h, moved, block)
            block = block.astype(BF16)
            dest, k = tile * own + d // chunks, d % chunks

            @pl.when(dest == me)
            def _():
                recv[k, me] = block

            @pl.when(dest != me)
            def _():
                pack[k, dest] = block
                if k == 0:
                    exchange(k, lax.rem(dest - me + n, n), pack, recv, send1, recv1).start()

    for k in range(1, chunks):

        @pl.loop(0, n - 1)
        def _(step):
            i = lax.rem(n // 2 + step, n - 1) + 1
            exchange(k, i, pack, recv, send1, recv1).start()

    loads[1].wait()
    for k in range(chunks):
        tok[k, 0:lead, :] = jnp.zeros((lead, LANES), F32)

        @pl.loop(0, total * p // LANES)
        def _(t):
            piece = filt[k * lc : (k + 1) * lc, lanes_of(t)].astype(F32)
            piece = jnp.concatenate([piece] * p, 0)
            tok[k, pl.ds(pl.multiple_of(lead + t * LANES, SUB), LANES), :] = piece.T

    for c in loads[2:]:
        c.wait()

    def group_rows(g):
        return pl.ds(pl.multiple_of(SUB * g, SUB), SUB)

    def filter_spectrum(k):
        @pl.loop(0, groups)
        def _(g):
            wide = []
            for b in range(p):
                col = []
                for a in range(half):
                    at = lead + b + p * (a * n2 + SUB * g)
                    now = tok[k, pl.ds(at, SUB, stride=p), :]
                    if b > 0:
                        old = tok[k, pl.ds(at - p, SUB, stride=p), :]
                        now = jnp.where(lane < b, old, now)
                    col.append(now)
                wide.append(jnp.concatenate(col, 0).astype(BF16))
            wide = jnp.concatenate(wide, 1)
            res = jnp.dot(first[g], wide, preferred_element_type=F32)
            spec_f[k, :, :, group_rows(g), :] = res.reshape(half, 2, SUB, p * LANES)

        @pl.loop(0, half)
        def _(s):
            x = spec_f[k, s].reshape(2 * n2, p * LANES).astype(BF16)
            z = jnp.dot(mid[jnp.minimum(s, 1)], x, preferred_element_type=F32)
            spec_f[k, s] = z.reshape(2, n2, p * LANES)

    def slabs(k, ss, which):
        x = jnp.concatenate([spec[s].reshape(2 * n2, LANES) for s in ss], 1).astype(BF16)
        z = jnp.dot(mid[which], x, preferred_element_type=F32)
        ys = []
        for j, s in enumerate(ss):
            zr = z[:n2, j * LANES : (j + 1) * LANES]
            zi = z[n2:, j * LANES : (j + 1) * LANES]
            rr = ii = cross = None
            for b in range(p):
                xr = zr if b == 0 else pltpu.roll(zr, b * lc, 1)
                xi = zi if b == 0 else pltpu.roll(zi, b * lc, 1)
                gr = spec_f[k, s, 0, :, b * LANES : (b + 1) * LANES]
                gi = spec_f[k, s, 1, :, b * LANES : (b + 1) * LANES]
                add = lambda t, v: v if t is None else t + v
                rr = add(rr, xr * gr)
                ii = add(ii, xi * gi)
                cross = add(cross, xr * gi + xi * gr)
            if which == 0:
                top = lax.broadcasted_iota(jnp.int32, (n2, LANES), 0) == 0
                yr = jnp.where(top, rr, rr - ii)
                yi = jnp.where(top, ii, cross)
            else:
                yr, yi = rr - ii, cross
            ys.append(jnp.concatenate((yr, yi), 0).astype(BF16))
        v = jnp.dot(back[which], jnp.concatenate(ys, 1), preferred_element_type=F32)
        for j, s in enumerate(ss):
            spec[s] = v[:, j * LANES : (j + 1) * LANES].reshape(2, n2, LANES)

    def block_rows(j):
        return pl.ds(pl.multiple_of(j * rpd, SUB), rpd)

    def convolve(k):
        sig[block_rows(me), :] = recv[k, me].astype(F32)

        @pl.loop(0, n - 1)
        def _(step):
            i = lax.rem(n // 2 + step, n - 1) + 1
            exchange(k, i, pack, recv, send1, recv1).wait_recv()
            j = lax.rem(me - i + n, n)
            sig[block_rows(j), :] = recv[k, j].astype(F32)

        @pl.loop(0, groups, unroll=2)
        def _(g):
            x = jnp.concatenate(
                [sig[pl.ds(pl.multiple_of(a * n2 + SUB * g, SUB), SUB), :] for a in range(half)], 0
            ).astype(BF16)
            res = jnp.dot(first[g], x, preferred_element_type=F32)
            spec[:, :, group_rows(g), :] = res.reshape(half, 2, SUB, LANES)

        slabs(k, [0], 0)
        slabs(k, [1], 1)

        @pl.loop(1, half // 2, unroll=2)
        def _(t):
            slabs(k, [2 * t, 2 * t + 1], 1)

        direct = jnp.concatenate([skip[:, k * lc : (k + 1) * lc]] * p, 1)

        @pl.loop(0, groups, unroll=2)
        def _(g):
            v = spec[:, :, group_rows(g), :].reshape(2 * half * SUB, LANES).astype(BF16)
            y = jnp.dot(last[g], v, preferred_element_type=F32)
            for a in range(half):
                at = pl.ds(pl.multiple_of(a * n2 + SUB * g, SUB), SUB)
                sig[at, :] = y[a * SUB : (a + 1) * SUB] + direct * sig[at, :]

        ret[k, me] = sig[block_rows(me), :].astype(BF16)

        @pl.loop(0, n - 1)
        def _(step):
            i = lax.rem(n // 2 + step, n - 1) + 1
            j = lax.rem(me + i, n)
            done[k, j] = sig[block_rows(j), :].astype(BF16)
            exchange(k, i, done, ret, send2, recv2).start()

    for k in range(chunks):
        filter_spectrum(k)
    for k in range(chunks):
        convolve(k)

    @pl.when(me < n - 1)
    def _():
        m_copy.wait_send()

    for k in range(chunks):

        @pl.loop(1, n)
        def _(i):
            exchange(k, i, pack, recv, send1, recv1).wait_send()
            exchange(k, i, done, ret, send2, recv2).wait()

    @pl.loop(0, tiles)
    def _(tile):
        parts = [ret[d % chunks, tile * own + d // chunks].astype(F32) for d in range(p)]
        for h in range(p):
            block = None
            for d in range(p):
                shift = ((d - h) % p) * lc
                moved = parts[d] if shift == 0 else pltpu.roll(parts[d], shift, 1)
                block = moved if block is None else jnp.where(lane == d, moved, block)
            drive[tile, pl.ds(h, rpd, stride=p), :] = block
        out[:, lanes_of(tile)] = (query[tile] * drive[tile]).astype(BF16)


def body(n, projected, taps, filters, skip):
    rows, _, chans = projected.shape
    lc, length = filters.shape
    chunks, sc, p = plan(chans, lc, n)
    rpd = rows // p
    total = length // p
    n1, n2 = factors(2 * total)
    half = n1 // 2
    tables = [jnp.asarray(t) for t in dft_tables(2 * total)]
    vmem = pl.BlockSpec(memory_space=pltpu.VMEM)
    hbm = pl.BlockSpec(memory_space=pl.ANY)
    sems = pltpu.SemaphoreType.DMA((chunks, n))
    blocks = pltpu.VMEM((chunks, n, rpd, LANES), BF16)
    moved = jnp.transpose(projected, (1, 0, 2))
    return pl.pallas_call(
        functools.partial(kernel, n, chunks),
        out_shape=jax.ShapeDtypeStruct((rows, chans), BF16),
        in_specs=[hbm, vmem, hbm, vmem] + [hbm] * 4,
        out_specs=vmem,
        scratch_shapes=[
            pltpu.VMEM(moved.shape, BF16),
            pltpu.VMEM(filters.shape, BF16),
            *[pltpu.VMEM(t.shape, BF16) for t in tables],
            pltpu.VMEM((3, 16, chans), BF16),
            pltpu.VMEM((chans // LANES, rows, LANES), F32),
            pltpu.VMEM((chans // LANES, rows, LANES), F32),
            blocks,
            blocks,
            pltpu.VMEM((total, LANES), F32),
            pltpu.VMEM((chunks, max(p, SUB) + length, LANES), F32),
            pltpu.VMEM((chunks, half, 2, n2, p * LANES), F32),
            pltpu.VMEM((half, 2, n2, LANES), F32),
            blocks,
            blocks,
            pltpu.SemaphoreType.DMA((6,)),
            pltpu.SemaphoreType.DMA,
            pltpu.SemaphoreType.DMA,
            sems, sems, sems, sems,
        ],
        compiler_params=pltpu.CompilerParams(
            collective_id=0, has_side_effects=True, vmem_limit_bytes=56 * 1024 * 1024
        ),
    )(moved, taps, filters, skip.reshape(1, lc), *tables)


def solution(mesh):
    placed = (P(("grp", "seq"), None, None), P(), P("seq", None), P("seq"))
    return jax.shard_map(
        functools.partial(body, mesh.shape["seq"]),
        mesh=mesh, in_specs=placed, out_specs=P(("grp", "seq"), None), check_vma=False,
    )
```

```python
import functools
import math

import jax
import jax.numpy as jnp
import numpy as np
from jax import lax
from jax.experimental import pallas as pl
from jax.experimental.pallas import tpu as pltpu
from jax.sharding import PartitionSpec as P

LANES = 128
SUB = 8
MAX_PHASES = 4
F32 = jnp.float32
BF16 = jnp.bfloat16


def factors(order):
    inner = 1 << ((int(math.log2(order)) + 1) // 2)
    return order // inner, inner


def dft_tables(order):
    n1, n2 = factors(order)
    half, hb = n1 // 2, n2 // 2
    groups = n2 // SUB
    s = np.arange(half)[:, None, None]
    a = np.arange(half)[None, :, None]
    b = np.arange(n2)[None, None, :]
    theta = 2 * np.pi * ((s * (a * n2 + b)) % order) / order
    sign = np.broadcast_to((-1.0) ** np.arange(half)[:, None], (half, n2))
    fwd = np.stack((np.cos(theta), -np.sin(theta)), 1)
    fwd[0, 0] = 1.0
    fwd[0, 1] = sign
    inv = np.stack((2 * np.cos(theta), -2 * np.sin(theta)), 1)
    inv[0, 0] = 1.0
    inv[0, 1] = sign
    inv = inv / order
    eye = np.eye(SUB)
    fwd_g = fwd.reshape(half, 2, half, groups, SUB)
    first = np.einsum("srage,ef->gsreaf", fwd_g, eye).reshape(groups, 2 * half * SUB, half * SUB)
    inv_g = inv.reshape(half, 2, half, groups, SUB)
    last = np.einsum("srage,ef->gaesrf", inv_g, eye).reshape(groups, half * SUB, 2 * half * SUB)
    k = np.arange(n2)
    phi = 2 * np.pi * (np.outer(k, k) % n2) / n2
    c, d = np.cos(phi), np.sin(phi)
    mid = np.block([[c, d], [-d, c]])
    back = np.block([[c, -d], [d, c]])
    kh = np.arange(hb)
    low = 2 * np.pi * (np.outer(kh, k) % n2) / n2
    odd = 2 * np.pi * (np.outer(half + n1 * kh, k) % order) / order
    mid0 = np.zeros((2 * n2, 2 * n2))
    mid0[:hb, :n2] = np.cos(low)
    mid0[hb:n2, n2:] = np.cos(odd)
    mid0[n2 : n2 + hb, :n2] = -np.sin(low)
    mid0[n2, :n2] = (-1.0) ** k
    mid0[n2 + hb :, n2:] = -np.sin(odd)
    back0 = 2 * mid0.T
    back0[:, 0] /= 2
    back0[:, n2] /= 2
    cast = lambda x: np.ascontiguousarray(x.astype(BF16))
    return cast(first), cast(np.stack((mid0, mid))), cast(np.stack((back0, back))), cast(last)


def plan(chans, lc, n):
    chunks = max(1, MAX_PHASES * lc // LANES)
    lc = lc // chunks
    return chunks, lc, LANES // lc


def kernel(
    n, chunks,
    proj_hbm, taps, filt_hbm, skip, first_hbm, mid_hbm, back_hbm, last_hbm,
    out,
    proj, filt, first, mid, back, last,
    margin, query, drive, pack, recv, sig, tok, spec_f, spec, done, ret,
    load, m_send, m_recv, send1, recv1, send2, recv2,
):
    me = lax.axis_index("seq")
    _, rows, chans = proj.shape
    count = taps.shape[0]
    lc = chans // n // chunks
    p = LANES // lc
    rpd = rows // p
    total = rpd * n
    n1, n2 = factors(2 * total)
    half = n1 // 2
    groups = n2 // SUB
    tiles = chans // LANES
    own = p // chunks
    mrows = margin.shape[1]
    lane = lax.broadcasted_iota(jnp.int32, (1, LANES), 1) // lc

    loads = [
        pltpu.make_async_copy(a, b, load.at[k])
        for k, (a, b) in enumerate(
            ((proj_hbm, proj), (filt_hbm, filt), (first_hbm, first), (mid_hbm, mid), (back_hbm, back), (last_hbm, last))
        )
    ]
    for c in loads:
        c.start()

    barrier = pltpu.get_barrier_semaphore()

    @pl.loop(1, n)
    def _(i):
        pl.semaphore_signal(barrier, inc=1, device_id={"seq": lax.rem(me + i, n)})

    def lanes_of(tile):
        return pl.ds(pl.multiple_of(tile * LANES, LANES), LANES)

    def features(tile, ext, many):
        feats = []
        for m in range(3):
            x = ext(m)
            from_row = x.shape[0] - many
            acc = None
            for o in range(count):
                term = taps[o, m : m + 1, lanes_of(tile)] * x[from_row - o : from_row - o + many]
                acc = term if acc is None else acc + term
            feats.append(acc)
        return feats[0], (feats[1] * feats[2]).astype(BF16).astype(F32)

    def tile_features(tile):
        zero = jnp.zeros((SUB, LANES), F32)
        q, d = features(
            tile, lambda m: jnp.concatenate((zero, proj[m, :, lanes_of(tile)].astype(F32)), 0), rows
        )
        query[tile] = q
        drive[tile] = d

    loads[0].wait()
    pl.loop(0, tiles // 2)(tile_features)

    pl.semaphore_wait(barrier, n - 1)
    m_copy = pltpu.make_async_remote_copy(
        src_ref=proj.at[:, pl.ds(rows - mrows, mrows)],
        dst_ref=margin,
        send_sem=m_send,
        recv_sem=m_recv,
        device_id={"seq": lax.rem(me + 1, n)},
    )

    @pl.when(me < n - 1)
    def _():
        m_copy.start()

    pl.loop(tiles // 2, tiles)(tile_features)

    @pl.when(me > 0)
    def _():
        m_copy.wait_recv()

    @pl.when(me == 0)
    def _():
        margin[...] = jnp.zeros_like(margin)

    def exchange(k, i, src, dst, ssem, rsem):
        return pltpu.make_async_remote_copy(
            src_ref=src.at[k, lax.rem(me + i, n)],
            dst_ref=dst.at[k, me],
            send_sem=ssem.at[k, i],
            recv_sem=rsem.at[k, i],
            device_id={"seq": lax.rem(me + i, n)},
        )

    @pl.loop(0, tiles, unroll=2)
    def _(step):
        tile = lax.rem(me // own + tiles // 2 + step, tiles)

        def ext(m):
            before = margin[m, :, lanes_of(tile)].astype(F32)
            after = proj[m, 0:16, lanes_of(tile)].astype(F32)
            return jnp.concatenate((before[mrows - SUB :], after[:SUB]), 0)

        q, dr = features(tile, ext, SUB)
        query[tile, 0:SUB] = q
        drive[tile, 0:SUB] = dr
        parts = [drive[tile, pl.ds(h, rpd, stride=p), :] for h in range(p)]
        for d in range(p):
            block = None
            for h in range(p):
                shift = ((h - d) % p) * lc
                moved = parts[h] if shift == 0 else pltpu.roll(parts[h], shift, 1)
                block = moved if block is None else jnp.where(lane == h, moved, block)
            block = block.astype(BF16)
            dest, k = tile * own + d // chunks, d % chunks

            @pl.when(dest == me)
            def _():
                recv[k, me] = block

            @pl.when(dest != me)
            def _():
                pack[k, dest] = block
                if k == 0:
                    exchange(k, lax.rem(dest - me + n, n), pack, recv, send1, recv1).start()

    for k in range(1, chunks):

        @pl.loop(0, n - 1)
        def _(step):
            i = lax.rem(n // 2 + step, n - 1) + 1
            exchange(k, i, pack, recv, send1, recv1).start()

    loads[1].wait()
    seg = LANES // p
    row_id = lax.broadcasted_iota(jnp.int32, (LANES, LANES), 0)
    col_id = lax.broadcasted_iota(jnp.int32, (LANES, LANES), 1)
    apart = (col_id == p * lax.rem(row_id, seg) + row_id // seg).astype(F32).astype(BF16)
    for k in range(chunks):
        for b in range(p):
            tok[k, b, 0:SUB, :] = jnp.zeros((SUB, LANES), F32)

    @pl.loop(0, total // seg, unroll=4)
    def _(t):
        piece = filt[:, lanes_of(t)]
        wide = jnp.concatenate([piece[k * lc : (k + 1) * lc] for k in range(chunks) for _ in range(p)], 0)
        turned = lax.dot_general(apart, wide, (((1,), (1,)), ((), ())), preferred_element_type=F32)
        for k in range(chunks):
            for b in range(p):
                at = pl.ds(pl.multiple_of(SUB + t * seg, SUB), seg)
                tok[k, b, at, :] = turned[b * seg : (b + 1) * seg, k * LANES : (k + 1) * LANES]

    for c in loads[2:]:
        c.wait()

    def group_rows(g):
        return pl.ds(pl.multiple_of(SUB * g, SUB), SUB)

    def filter_spectrum(k):
        @pl.loop(0, groups, unroll=2)
        def _(g):
            wide = []
            for b in range(p):
                col = []
                for a in range(half):
                    at = a * n2 + SUB * g
                    now = tok[k, b, pl.ds(pl.multiple_of(SUB + at, SUB), SUB), :]
                    if b > 0:
                        old = tok[k, b, pl.ds(SUB - 1 + at, SUB), :]
                        now = jnp.where(lane < b, old, now)
                    col.append(now)
                wide.append(jnp.concatenate(col, 0).astype(BF16))
            wide = jnp.concatenate(wide, 1)
            res = jnp.dot(first[g], wide, preferred_element_type=F32)
            spec_f[k, :, :, group_rows(g), :] = res.reshape(half, 2, SUB, p * LANES)

        @pl.loop(0, half, unroll=4)
        def _(s):
            x = spec_f[k, s].reshape(2 * n2, p * LANES).astype(BF16)
            z = jnp.dot(mid[jnp.minimum(s, 1)], x, preferred_element_type=F32)
            spec_f[k, s] = z.reshape(2, n2, p * LANES)

    def slabs(k, ss, which):
        x = jnp.concatenate([spec[s].reshape(2 * n2, LANES) for s in ss], 1).astype(BF16)
        z = jnp.dot(mid[which], x, preferred_element_type=F32)
        ys = []
        for j, s in enumerate(ss):
            zr = z[:n2, j * LANES : (j + 1) * LANES]
            zi = z[n2:, j * LANES : (j + 1) * LANES]
            rr = ii = cross = None
            for b in range(p):
                xr = zr if b == 0 else pltpu.roll(zr, b * lc, 1)
                xi = zi if b == 0 else pltpu.roll(zi, b * lc, 1)
                gr = spec_f[k, s, 0, :, b * LANES : (b + 1) * LANES]
                gi = spec_f[k, s, 1, :, b * LANES : (b + 1) * LANES]
                add = lambda t, v: v if t is None else t + v
                rr = add(rr, xr * gr)
                ii = add(ii, xi * gi)
                cross = add(cross, xr * gi + xi * gr)
            if which == 0:
                top = lax.broadcasted_iota(jnp.int32, (n2, LANES), 0) == 0
                yr = jnp.where(top, rr, rr - ii)
                yi = jnp.where(top, ii, cross)
            else:
                yr, yi = rr - ii, cross
            ys.append(jnp.concatenate((yr, yi), 0).astype(BF16))
        v = jnp.dot(back[which], jnp.concatenate(ys, 1), preferred_element_type=F32)
        for j, s in enumerate(ss):
            spec[s] = v[:, j * LANES : (j + 1) * LANES].reshape(2, n2, LANES)

    def block_rows(j):
        return pl.ds(pl.multiple_of(j * rpd, SUB), rpd)

    def convolve(k):
        sig[block_rows(me), :] = recv[k, me].astype(F32)

        @pl.loop(0, n - 1)
        def _(step):
            i = lax.rem(n // 2 + step, n - 1) + 1
            exchange(k, i, pack, recv, send1, recv1).wait_recv()
            j = lax.rem(me - i + n, n)
            sig[block_rows(j), :] = recv[k, j].astype(F32)

        @pl.loop(0, groups, unroll=4)
        def _(g):
            x = jnp.concatenate(
                [sig[pl.ds(pl.multiple_of(a * n2 + SUB * g, SUB), SUB), :] for a in range(half)], 0
            ).astype(BF16)
            res = jnp.dot(first[g], x, preferred_element_type=F32)
            spec[:, :, group_rows(g), :] = res.reshape(half, 2, SUB, LANES)

        slabs(k, [0], 0)
        slabs(k, [1], 1)

        @pl.loop(1, half // 2, unroll=half // 2 - 1)
        def _(t):
            slabs(k, [2 * t, 2 * t + 1], 1)

        direct = jnp.concatenate([skip[:, k * lc : (k + 1) * lc]] * p, 1)

        @pl.loop(0, groups, unroll=4)
        def _(g):
            v = spec[:, :, group_rows(g), :].reshape(2 * half * SUB, LANES).astype(BF16)
            y = jnp.dot(last[g], v, preferred_element_type=F32)
            for a in range(half):
                at = pl.ds(pl.multiple_of(a * n2 + SUB * g, SUB), SUB)
                sig[at, :] = y[a * SUB : (a + 1) * SUB] + direct * sig[at, :]

        ret[k, me] = sig[block_rows(me), :].astype(BF16)

        @pl.loop(0, n - 1)
        def _(step):
            i = lax.rem(n // 2 + step, n - 1) + 1
            j = lax.rem(me + i, n)
            done[k, j] = sig[block_rows(j), :].astype(BF16)
            exchange(k, i, done, ret, send2, recv2).start()

    for k in range(chunks):
        filter_spectrum(k)
    for k in range(chunks):
        convolve(k)

    @pl.when(me < n - 1)
    def _():
        m_copy.wait_send()

    for k in range(chunks):

        @pl.loop(1, n)
        def _(i):
            exchange(k, i, pack, recv, send1, recv1).wait_send()
            exchange(k, i, done, ret, send2, recv2).wait()

    @pl.loop(0, tiles, unroll=2)
    def _(tile):
        parts = [ret[d % chunks, tile * own + d // chunks].astype(F32) for d in range(p)]
        for h in range(p):
            block = None
            for d in range(p):
                shift = ((d - h) % p) * lc
                moved = parts[d] if shift == 0 else pltpu.roll(parts[d], shift, 1)
                block = moved if block is None else jnp.where(lane == d, moved, block)
            drive[tile, pl.ds(h, rpd, stride=p), :] = block
        out[:, lanes_of(tile)] = (query[tile] * drive[tile]).astype(BF16)


def body(n, projected, taps, filters, skip):
    rows, _, chans = projected.shape
    lc, length = filters.shape
    chunks, sc, p = plan(chans, lc, n)
    rpd = rows // p
    total = length // p
    n1, n2 = factors(2 * total)
    half = n1 // 2
    tables = [jnp.asarray(t) for t in dft_tables(2 * total)]
    vmem = pl.BlockSpec(memory_space=pltpu.VMEM)
    hbm = pl.BlockSpec(memory_space=pl.ANY)
    sems = pltpu.SemaphoreType.DMA((chunks, n))
    blocks = pltpu.VMEM((chunks, n, rpd, LANES), BF16)
    moved = jnp.transpose(projected, (1, 0, 2))
    return pl.pallas_call(
        functools.partial(kernel, n, chunks),
        out_shape=jax.ShapeDtypeStruct((rows, chans), BF16),
        in_specs=[hbm, vmem, hbm, vmem] + [hbm] * 4,
        out_specs=vmem,
        scratch_shapes=[
            pltpu.VMEM(moved.shape, BF16),
            pltpu.VMEM(filters.shape, BF16),
            *[pltpu.VMEM(t.shape, BF16) for t in tables],
            pltpu.VMEM((3, 16, chans), BF16),
            pltpu.VMEM((chans // LANES, rows, LANES), F32),
            pltpu.VMEM((chans // LANES, rows, LANES), F32),
            blocks,
            blocks,
            pltpu.VMEM((total, LANES), F32),
            pltpu.VMEM((chunks, p, SUB + total, LANES), F32),
            pltpu.VMEM((chunks, half, 2, n2, p * LANES), F32),
            pltpu.VMEM((half, 2, n2, LANES), F32),
            blocks,
            blocks,
            pltpu.SemaphoreType.DMA((6,)),
            pltpu.SemaphoreType.DMA,
            pltpu.SemaphoreType.DMA,
            sems, sems, sems, sems,
        ],
        compiler_params=pltpu.CompilerParams(
            collective_id=0, has_side_effects=True, vmem_limit_bytes=56 * 1024 * 1024
        ),
    )(moved, taps, filters, skip.reshape(1, lc), *tables)


def solution(mesh):
    placed = (P(("grp", "seq"), None, None), P(), P("seq", None), P("seq"))
    return jax.shard_map(
        functools.partial(body, mesh.shape["seq"]),
        mesh=mesh, in_specs=placed, out_specs=P(("grp", "seq"), None), check_vma=False,
    )
```

```python
import functools
import math

import jax
import jax.numpy as jnp
import numpy as np
from jax import lax
from jax.experimental import pallas as pl
from jax.experimental.pallas import tpu as pltpu
from jax.sharding import PartitionSpec as P

LANES = 128
SUB = 8
GROUP = 16
MAX_PHASES = 4
F32 = jnp.float32
BF16 = jnp.bfloat16


def factors(order):
    inner = 1 << ((int(math.log2(order)) + 1) // 2)
    return order // inner, inner


def dft_tables(order):
    n1, n2 = factors(order)
    half, hb = n1 // 2, n2 // 2
    groups = n2 // GROUP
    s = np.arange(half)[:, None, None]
    a = np.arange(half)[None, :, None]
    b = np.arange(n2)[None, None, :]
    theta = 2 * np.pi * ((s * (a * n2 + b)) % order) / order
    sign = np.broadcast_to((-1.0) ** np.arange(half)[:, None], (half, n2))
    fwd = np.stack((np.cos(theta), -np.sin(theta)), 1)
    fwd[0, 0] = 1.0
    fwd[0, 1] = sign
    inv = np.stack((2 * np.cos(theta), -2 * np.sin(theta)), 1)
    inv[0, 0] = 1.0
    inv[0, 1] = sign
    inv = inv / order
    eye = np.eye(GROUP)
    fwd_g = fwd.reshape(half, 2, half, groups, GROUP)
    first = np.einsum("srage,ef->gsreaf", fwd_g, eye).reshape(groups, 2 * half * GROUP, half * GROUP)
    inv_g = inv.reshape(half, 2, half, groups, GROUP)
    last = np.einsum("srage,ef->gaesrf", inv_g, eye).reshape(groups, half * GROUP, 2 * half * GROUP)
    k = np.arange(n2)
    phi = 2 * np.pi * (np.outer(k, k) % n2) / n2
    c, d = np.cos(phi), np.sin(phi)
    mid = np.block([[c, d], [-d, c]])
    back = np.block([[c, -d], [d, c]])
    kh = np.arange(hb)
    low = 2 * np.pi * (np.outer(kh, k) % n2) / n2
    odd = 2 * np.pi * (np.outer(half + n1 * kh, k) % order) / order
    mid0 = np.zeros((2 * n2, 2 * n2))
    mid0[:hb, :n2] = np.cos(low)
    mid0[hb:n2, n2:] = np.cos(odd)
    mid0[n2 : n2 + hb, :n2] = -np.sin(low)
    mid0[n2, :n2] = (-1.0) ** k
    mid0[n2 + hb :, n2:] = -np.sin(odd)
    back0 = 2 * mid0.T
    back0[:, 0] /= 2
    back0[:, n2] /= 2
    cast = lambda x: np.ascontiguousarray(x.astype(BF16))
    return cast(first), cast(np.stack((mid0, mid))), cast(np.stack((back0, back))), cast(last)


def plan(chans, lc, n):
    chunks = max(1, MAX_PHASES * lc // LANES)
    lc = lc // chunks
    return chunks, lc, LANES // lc


def kernel(
    n, chunks,
    proj_hbm, taps, filt_hbm, skip, first_hbm, mid_hbm, back_hbm, last_hbm,
    out,
    proj, filt, first, mid, back, last,
    margin, query, drive, pack, recv, tok, wide_f, spec_f, spec, done, ret,
    load, m_send, m_recv, send1, recv1, send2, recv2,
):
    me = lax.axis_index("seq")
    _, rows, chans = proj.shape
    count = taps.shape[0]
    lc = chans // n // chunks
    p = LANES // lc
    rpd = rows // p
    total = rpd * n
    n1, n2 = factors(2 * total)
    half = n1 // 2
    groups = n2 // GROUP
    tiles = chans // LANES
    own = p // chunks
    mrows = margin.shape[1]
    lane = lax.broadcasted_iota(jnp.int32, (1, LANES), 1) // lc

    loads = [
        pltpu.make_async_copy(a, b, load.at[k])
        for k, (a, b) in enumerate(
            ((proj_hbm, proj), (filt_hbm, filt.at[:, pl.ds(LANES, total * p)]), (first_hbm, first), (mid_hbm, mid), (back_hbm, back), (last_hbm, last))
        )
    ]
    for c in loads:
        c.start()

    barrier = pltpu.get_barrier_semaphore()

    @pl.loop(1, n)
    def _(i):
        pl.semaphore_signal(barrier, inc=1, device_id={"seq": lax.rem(me + i, n)})

    def lanes_of(tile):
        return pl.ds(pl.multiple_of(tile * LANES, LANES), LANES)

    def features(tile, ext, many):
        feats = []
        for m in range(3):
            x = ext(m)
            from_row = x.shape[0] - many
            acc = None
            for o in range(count):
                term = taps[o, m : m + 1, lanes_of(tile)] * x[from_row - o : from_row - o + many]
                acc = term if acc is None else acc + term
            feats.append(acc)
        return feats[0], (feats[1] * feats[2]).astype(BF16).astype(F32)

    def tile_features(tile):
        zero = jnp.zeros((SUB, LANES), F32)
        q, d = features(
            tile, lambda m: jnp.concatenate((zero, proj[m, :, lanes_of(tile)].astype(F32)), 0), rows
        )
        query[tile] = q
        drive[tile] = d

    loads[0].wait()
    pl.loop(0, tiles // 2)(tile_features)

    pl.semaphore_wait(barrier, n - 1)
    m_copy = pltpu.make_async_remote_copy(
        src_ref=proj.at[:, pl.ds(rows - mrows, mrows)],
        dst_ref=margin,
        send_sem=m_send,
        recv_sem=m_recv,
        device_id={"seq": lax.rem(me + 1, n)},
    )

    @pl.when(me < n - 1)
    def _():
        m_copy.start()

    pl.loop(tiles // 2, tiles)(tile_features)

    @pl.when(me > 0)
    def _():
        m_copy.wait_recv()

    @pl.when(me == 0)
    def _():
        margin[...] = jnp.zeros_like(margin)

    def block_rows(j):
        return pl.ds(pl.multiple_of(j * rpd, GROUP), rpd)

    def send_drive(k, i):
        dest = lax.rem(me + i, n)
        return pltpu.make_async_remote_copy(
            src_ref=pack.at[k, dest],
            dst_ref=recv.at[k, block_rows(me)],
            send_sem=send1.at[k, i],
            recv_sem=recv1.at[k, i],
            device_id={"seq": dest},
        )

    def send_long(k, i):
        dest = lax.rem(me + i, n)
        return pltpu.make_async_remote_copy(
            src_ref=done.at[k, block_rows(dest)],
            dst_ref=ret.at[k, me],
            send_sem=send2.at[k, i],
            recv_sem=recv2.at[k, i],
            device_id={"seq": dest},
        )

    @pl.loop(0, tiles, unroll=2)
    def _(step):
        tile = lax.rem(me // own + tiles // 2 + step, tiles)

        def ext(m):
            before = margin[m, :, lanes_of(tile)].astype(F32)
            after = proj[m, 0:16, lanes_of(tile)].astype(F32)
            return jnp.concatenate((before[mrows - SUB :], after[:SUB]), 0)

        q, dr = features(tile, ext, SUB)
        query[tile, 0:SUB] = q
        drive[tile, 0:SUB] = dr
        parts = [drive[tile, pl.ds(h, rpd, stride=p), :] for h in range(p)]
        for d in range(p):
            block = None
            for h in range(p):
                shift = ((h - d) % p) * lc
                moved = parts[h] if shift == 0 else pltpu.roll(parts[h], shift, 1)
                block = moved if block is None else jnp.where(lane == h, moved, block)
            block = block.astype(BF16)
            dest, k = tile * own + d // chunks, d % chunks

            @pl.when(dest == me)
            def _():
                recv[k, block_rows(me), :] = block

            @pl.when(dest != me)
            def _():
                pack[k, dest] = block
                if k == 0:
                    send_drive(k, lax.rem(dest - me + n, n)).start()

    for k in range(1, chunks):

        @pl.loop(0, n - 1)
        def _(step):
            i = lax.rem(n // 2 + step, n - 1) + 1
            send_drive(k, i).start()

    loads[1].wait()
    seg = LANES // p
    row_id = lax.broadcasted_iota(jnp.int32, (2 * LANES, 2 * LANES), 0)
    col_id = lax.broadcasted_iota(jnp.int32, (2 * LANES, 2 * LANES), 1)
    inside = lax.rem(row_id, LANES)
    source = LANES + p * lax.rem(inside, seg) + inside // seg - jnp.where(row_id < LANES, 0, p)
    apart = (col_id == source).astype(F32).astype(BF16)
    filt[:, 0:LANES] = jnp.zeros((filt.shape[0], LANES), BF16)

    @pl.loop(0, total // seg, unroll=4)
    def _(t):
        piece = filt[:, pl.ds(pl.multiple_of(t * LANES, LANES), 2 * LANES)]
        wide = jnp.concatenate([piece[k * lc : (k + 1) * lc] for k in range(chunks) for _ in range(p)], 0)
        turned = lax.dot_general(apart, wide, (((1,), (1,)), ((), ())), preferred_element_type=F32)
        at = pl.ds(pl.multiple_of(t * seg, GROUP), seg)
        for k in range(chunks):
            for b in range(p):
                now = turned[b * seg : (b + 1) * seg, k * LANES : (k + 1) * LANES]
                old = turned[LANES + b * seg : LANES + (b + 1) * seg, k * LANES : (k + 1) * LANES]
                tok[k, b, at, :] = jnp.where(lane < b, old, now).astype(BF16)

    for c in loads[2:]:
        c.wait()

    def group_rows(g, a=0):
        return pl.ds(pl.multiple_of(a * n2 + GROUP * g, GROUP), GROUP)

    def filter_spectrum(k):
        @pl.loop(0, groups, unroll=2)
        def _(g):
            wide = jnp.concatenate(
                [
                    jnp.concatenate([tok[k, b, group_rows(g, a), :] for a in range(half)], 0)
                    for b in range(p)
                ],
                1,
            )
            res = jnp.dot(first[g], wide, preferred_element_type=F32)
            wide_f[:, :, group_rows(g), :] = res.astype(BF16).reshape(half, 2, GROUP, p * LANES)

        def one(s, which):
            x = wide_f[s].reshape(2 * n2, p * LANES)
            z = jnp.dot(mid[which], x, preferred_element_type=F32)
            spec_f[s] = z.reshape(2, n2, p * LANES)

        one(0, 0)

        @pl.loop(1, half, unroll=5)
        def _(s):
            one(s, 1)

    def slabs(k, ss, which):
        x = jnp.concatenate([spec[s].reshape(2 * n2, LANES) for s in ss], 1)
        z = jnp.dot(mid[which], x, preferred_element_type=F32)
        ys = []
        for j, s in enumerate(ss):
            zr = z[:n2, j * LANES : (j + 1) * LANES]
            zi = z[n2:, j * LANES : (j + 1) * LANES]
            rr = ii = cross = None
            for b in range(p):
                xr = zr if b == 0 else pltpu.roll(zr, b * lc, 1)
                xi = zi if b == 0 else pltpu.roll(zi, b * lc, 1)
                gr = spec_f[s, 0, :, b * LANES : (b + 1) * LANES]
                gi = spec_f[s, 1, :, b * LANES : (b + 1) * LANES]
                add = lambda t, v: v if t is None else t + v
                rr = add(rr, xr * gr)
                ii = add(ii, xi * gi)
                cross = add(cross, xr * gi + xi * gr)
            if which == 0:
                top = lax.broadcasted_iota(jnp.int32, (n2, LANES), 0) == 0
                yr = jnp.where(top, rr, rr - ii)
                yi = jnp.where(top, ii, cross)
            else:
                yr, yi = rr - ii, cross
            ys.append(jnp.concatenate((yr, yi), 0).astype(BF16))
        v = jnp.dot(back[which], jnp.concatenate(ys, 1), preferred_element_type=F32)
        for j, s in enumerate(ss):
            spec[s] = v[:, j * LANES : (j + 1) * LANES].astype(BF16).reshape(2, n2, LANES)

    def convolve(k):
        @pl.loop(1, n)
        def _(i):
            send_drive(k, i).wait_recv()

        @pl.loop(0, groups, unroll=groups)
        def _(g):
            x = jnp.concatenate([recv[k, group_rows(g, a), :] for a in range(half)], 0)
            res = jnp.dot(first[g], x, preferred_element_type=F32)
            spec[:, :, group_rows(g), :] = res.astype(BF16).reshape(half, 2, GROUP, LANES)

        slabs(k, [0], 0)
        slabs(k, [1], 1)

        @pl.loop(1, half // 2, unroll=half // 2 - 1)
        def _(t):
            slabs(k, [2 * t, 2 * t + 1], 1)

        direct = jnp.concatenate([skip[:, k * lc : (k + 1) * lc]] * p, 1)

        @pl.loop(0, groups, unroll=groups)
        def _(g):
            v = spec[:, :, group_rows(g), :].reshape(2 * half * GROUP, LANES)
            y = jnp.dot(last[g], v, preferred_element_type=F32)
            for a in range(half):
                at = group_rows(g, a)
                both = y[a * GROUP : (a + 1) * GROUP] + direct * recv[k, at, :].astype(F32)
                done[k, at, :] = both.astype(BF16)

        ret[k, me] = done[k, block_rows(me), :]

        @pl.loop(0, n - 1)
        def _(step):
            send_long(k, lax.rem(n // 2 + step, n - 1) + 1).start()

    for k in range(chunks):
        filter_spectrum(k)
        convolve(k)

    @pl.when(me < n - 1)
    def _():
        m_copy.wait_send()

    for k in range(chunks):

        @pl.loop(1, n)
        def _(i):
            send_drive(k, i).wait_send()
            send_long(k, i).wait()

    @pl.loop(0, tiles, unroll=2)
    def _(tile):
        parts = [ret[d % chunks, tile * own + d // chunks].astype(F32) for d in range(p)]
        for h in range(p):
            block = None
            for d in range(p):
                shift = ((d - h) % p) * lc
                moved = parts[d] if shift == 0 else pltpu.roll(parts[d], shift, 1)
                block = moved if block is None else jnp.where(lane == d, moved, block)
            drive[tile, pl.ds(h, rpd, stride=p), :] = block
        out[:, lanes_of(tile)] = (query[tile] * drive[tile]).astype(BF16)


def body(n, projected, taps, filters, skip):
    rows, _, chans = projected.shape
    lc, length = filters.shape
    chunks, sc, p = plan(chans, lc, n)
    rpd = rows // p
    total = length // p
    n1, n2 = factors(2 * total)
    half = n1 // 2
    tables = [jnp.asarray(t) for t in dft_tables(2 * total)]
    vmem = pl.BlockSpec(memory_space=pltpu.VMEM)
    hbm = pl.BlockSpec(memory_space=pl.ANY)
    sems = pltpu.SemaphoreType.DMA((chunks, n))
    blocks = pltpu.VMEM((chunks, n, rpd, LANES), BF16)
    flat = pltpu.VMEM((chunks, total, LANES), BF16)
    moved = jnp.transpose(projected, (1, 0, 2))
    return pl.pallas_call(
        functools.partial(kernel, n, chunks),
        out_shape=jax.ShapeDtypeStruct((rows, chans), BF16),
        in_specs=[hbm, vmem, hbm, vmem] + [hbm] * 4,
        out_specs=vmem,
        scratch_shapes=[
            pltpu.VMEM(moved.shape, BF16),
            pltpu.VMEM((filters.shape[0], LANES + length), BF16),
            *[pltpu.VMEM(t.shape, BF16) for t in tables],
            pltpu.VMEM((3, 16, chans), BF16),
            pltpu.VMEM((chans // LANES, rows, LANES), F32),
            pltpu.VMEM((chans // LANES, rows, LANES), F32),
            blocks,
            flat,
            pltpu.VMEM((chunks, p, total, LANES), BF16),
            pltpu.VMEM((half, 2, n2, p * LANES), BF16),
            pltpu.VMEM((half, 2, n2, p * LANES), F32),
            pltpu.VMEM((half, 2, n2, LANES), BF16),
            flat,
            blocks,
            pltpu.SemaphoreType.DMA((6,)),
            pltpu.SemaphoreType.DMA,
            pltpu.SemaphoreType.DMA,
            sems, sems, sems, sems,
        ],
        compiler_params=pltpu.CompilerParams(
            collective_id=0, has_side_effects=True, vmem_limit_bytes=56 * 1024 * 1024
        ),
    )(moved, taps, filters, skip.reshape(1, lc), *tables)


def solution(mesh):
    placed = (P(("grp", "seq"), None, None), P(), P("seq", None), P("seq"))
    return jax.shard_map(
        functools.partial(body, mesh.shape["seq"]),
        mesh=mesh, in_specs=placed, out_specs=P(("grp", "seq"), None), check_vma=False,
    )
```

```python
import functools
import math

import jax
import jax.numpy as jnp
import numpy as np
from jax import lax
from jax.experimental import pallas as pl
from jax.experimental.pallas import tpu as pltpu
from jax.sharding import PartitionSpec as P

LANES = 128
SUB = 8
GROUP = 16
MAX_PHASES = 4
F32 = jnp.float32
BF16 = jnp.bfloat16


def factors(order):
    inner = 1 << ((int(math.log2(order)) + 1) // 2)
    return order // inner, inner


def dft_tables(order):
    n1, n2 = factors(order)
    half, hb = n1 // 2, n2 // 2
    groups = n2 // GROUP
    s = np.arange(half)[:, None, None]
    a = np.arange(half)[None, :, None]
    b = np.arange(n2)[None, None, :]
    theta = 2 * np.pi * ((s * (a * n2 + b)) % order) / order
    sign = np.broadcast_to((-1.0) ** np.arange(half)[:, None], (half, n2))
    fwd = np.stack((np.cos(theta), -np.sin(theta)), 1)
    fwd[0, 0] = 1.0
    fwd[0, 1] = sign
    inv = np.stack((2 * np.cos(theta), -2 * np.sin(theta)), 1)
    inv[0, 0] = 1.0
    inv[0, 1] = sign
    inv = inv / order
    eye = np.eye(GROUP)
    fwd_g = fwd.reshape(half, 2, half, groups, GROUP)
    first = np.einsum("srage,ef->gsreaf", fwd_g, eye).reshape(groups, 2 * half * GROUP, half * GROUP)
    inv_g = inv.reshape(half, 2, half, groups, GROUP)
    last = np.einsum("srage,ef->gaesrf", inv_g, eye).reshape(groups, half * GROUP, 2 * half * GROUP)
    k = np.arange(n2)
    phi = 2 * np.pi * (np.outer(k, k) % n2) / n2
    c, d = np.cos(phi), np.sin(phi)
    mid = np.block([[c, d], [-d, c]])
    back = np.block([[c, -d], [d, c]])
    kh = np.arange(hb)
    low = 2 * np.pi * (np.outer(kh, k) % n2) / n2
    odd = 2 * np.pi * (np.outer(half + n1 * kh, k) % order) / order
    mid0 = np.zeros((2 * n2, 2 * n2))
    mid0[:hb, :n2] = np.cos(low)
    mid0[hb:n2, n2:] = np.cos(odd)
    mid0[n2 : n2 + hb, :n2] = -np.sin(low)
    mid0[n2, :n2] = (-1.0) ** k
    mid0[n2 + hb :, n2:] = -np.sin(odd)
    back0 = 2 * mid0.T
    back0[:, 0] /= 2
    back0[:, n2] /= 2
    cast = lambda x: np.ascontiguousarray(x.astype(BF16))
    return cast(first), cast(np.stack((mid0, mid))), cast(np.stack((back0, back))), cast(last)


def plan(chans, lc, n):
    chunks = max(1, MAX_PHASES * lc // LANES)
    lc = lc // chunks
    return chunks, lc, LANES // lc


def kernel(
    n, chunks,
    proj_hbm, taps, filt_hbm, skip, first_hbm, mid_hbm, back_hbm, last_hbm,
    out,
    proj, filt, first, mid, back, last,
    margin, query, drive, pack, recv, tok, wide_f, spec_f, spec, done, ret,
    load, m_send, m_recv, send1, recv1, send2, recv2,
):
    me = lax.axis_index("seq")
    _, rows, chans = proj.shape
    count = taps.shape[0]
    lc = chans // n // chunks
    p = LANES // lc
    rpd = rows // p
    total = rpd * n
    n1, n2 = factors(2 * total)
    half = n1 // 2
    groups = n2 // GROUP
    tiles = chans // LANES
    own = p // chunks
    mrows = margin.shape[1]
    lane = lax.broadcasted_iota(jnp.int32, (1, LANES), 1) // lc

    loads = [
        pltpu.make_async_copy(a, b, load.at[k])
        for k, (a, b) in enumerate(
            ((proj_hbm, proj), (filt_hbm, filt.at[:, pl.ds(LANES, total * p)]), (first_hbm, first), (mid_hbm, mid), (back_hbm, back), (last_hbm, last))
        )
    ]
    for c in loads:
        c.start()

    barrier = pltpu.get_barrier_semaphore()

    @pl.loop(1, n)
    def _(i):
        pl.semaphore_signal(barrier, inc=1, device_id={"seq": lax.rem(me + i, n)})

    def lanes_of(tile):
        return pl.ds(pl.multiple_of(tile * LANES, LANES), LANES)

    def features(tile, ext, many):
        feats = []
        for m in range(3):
            x = ext(m)
            from_row = x.shape[0] - many
            acc = None
            for o in range(count):
                term = taps[o, m : m + 1, lanes_of(tile)] * x[from_row - o : from_row - o + many]
                acc = term if acc is None else acc + term
            feats.append(acc)
        return feats[0], (feats[1] * feats[2]).astype(BF16).astype(F32)

    def tile_at(step):
        return lax.rem(me // own + tiles // 2 + step, tiles)

    def tile_features(step):
        tile = tile_at(step)
        zero = jnp.zeros((SUB, LANES), F32)
        q, d = features(
            tile, lambda m: jnp.concatenate((zero, proj[m, :, lanes_of(tile)].astype(F32)), 0), rows
        )
        query[tile] = q
        drive[tile] = d

    loads[0].wait()
    pl.loop(0, tiles // 2)(tile_features)

    pl.semaphore_wait(barrier, n - 1)
    m_copy = pltpu.make_async_remote_copy(
        src_ref=proj.at[:, pl.ds(rows - mrows, mrows)],
        dst_ref=margin,
        send_sem=m_send,
        recv_sem=m_recv,
        device_id={"seq": lax.rem(me + 1, n)},
    )

    @pl.when(me < n - 1)
    def _():
        m_copy.start()

    early = 3 * tiles // 4
    pl.loop(tiles // 2, early)(tile_features)

    @pl.when(me > 0)
    def _():
        m_copy.wait_recv()

    @pl.when(me == 0)
    def _():
        margin[...] = jnp.zeros_like(margin)

    def block_rows(j):
        return pl.ds(pl.multiple_of(j * rpd, GROUP), rpd)

    def send_drive(k, i):
        dest = lax.rem(me + i, n)
        return pltpu.make_async_remote_copy(
            src_ref=pack.at[k, dest],
            dst_ref=recv.at[k, block_rows(me)],
            send_sem=send1.at[k, i],
            recv_sem=recv1.at[k, i],
            device_id={"seq": dest},
        )

    def send_long(k, i):
        dest = lax.rem(me + i, n)
        return pltpu.make_async_remote_copy(
            src_ref=done.at[k, block_rows(dest)],
            dst_ref=ret.at[k, me],
            send_sem=send2.at[k, i],
            recv_sem=recv2.at[k, i],
            device_id={"seq": dest},
        )

    def send_tile(step):
        tile = tile_at(step)

        def ext(m):
            before = margin[m, :, lanes_of(tile)].astype(F32)
            after = proj[m, 0:16, lanes_of(tile)].astype(F32)
            return jnp.concatenate((before[mrows - SUB :], after[:SUB]), 0)

        q, dr = features(tile, ext, SUB)
        query[tile, 0:SUB] = q
        drive[tile, 0:SUB] = dr
        parts = [drive[tile, pl.ds(h, rpd, stride=p), :] for h in range(p)]
        for d in range(p):
            block = None
            for h in range(p):
                shift = ((h - d) % p) * lc
                moved = parts[h] if shift == 0 else pltpu.roll(parts[h], shift, 1)
                block = moved if block is None else jnp.where(lane == h, moved, block)
            block = block.astype(BF16)
            dest, k = tile * own + d // chunks, d % chunks

            @pl.when(dest == me)
            def _():
                recv[k, block_rows(me), :] = block

            @pl.when(dest != me)
            def _():
                pack[k, dest] = block
                if k == 0:
                    send_drive(k, lax.rem(dest - me + n, n)).start()

    pl.loop(0, early, unroll=2)(send_tile)

    @pl.loop(early, tiles)
    def _(step):
        tile_features(step)
        send_tile(step)

    def offset(step):
        return lax.rem(n // 2 + step, n - 1) + 1

    def follow(k, lo, hi):
        if k + 1 < chunks:

            @pl.loop(lo, hi)
            def _(step):
                send_drive(k, offset(step)).wait_send()
                send_drive(k + 1, offset(step)).start()

    loads[1].wait()
    seg = LANES // p
    row_id = lax.broadcasted_iota(jnp.int32, (2 * LANES, 2 * LANES), 0)
    col_id = lax.broadcasted_iota(jnp.int32, (2 * LANES, 2 * LANES), 1)
    inside = lax.rem(row_id, LANES)
    source = LANES + p * lax.rem(inside, seg) + inside // seg - jnp.where(row_id < LANES, 0, p)
    apart = (col_id == source).astype(F32).astype(BF16)
    filt[:, 0:LANES] = jnp.zeros((filt.shape[0], LANES), BF16)

    @pl.loop(0, total // seg, unroll=4)
    def _(t):
        piece = filt[:, pl.ds(pl.multiple_of(t * LANES, LANES), 2 * LANES)]
        wide = jnp.concatenate([piece[k * lc : (k + 1) * lc] for k in range(chunks) for _ in range(p)], 0)
        turned = lax.dot_general(apart, wide, (((1,), (1,)), ((), ())), preferred_element_type=F32)
        at = pl.ds(pl.multiple_of(t * seg, GROUP), seg)
        for k in range(chunks):
            for b in range(p):
                now = turned[b * seg : (b + 1) * seg, k * LANES : (k + 1) * LANES]
                old = turned[LANES + b * seg : LANES + (b + 1) * seg, k * LANES : (k + 1) * LANES]
                tok[k, b, at, :] = jnp.where(lane < b, old, now).astype(BF16)

    for c in loads[2:]:
        c.wait()

    def group_rows(g, a=0):
        return pl.ds(pl.multiple_of(a * n2 + GROUP * g, GROUP), GROUP)

    def filter_spectrum(k):
        follow(k, 0, n // 2)

        @pl.loop(0, groups, unroll=2)
        def _(g):
            wide = jnp.concatenate(
                [
                    jnp.concatenate([tok[k, b, group_rows(g, a), :] for a in range(half)], 0)
                    for b in range(p)
                ],
                1,
            )
            res = jnp.dot(first[g], wide, preferred_element_type=F32)
            wide_f[:, :, group_rows(g), :] = res.astype(BF16).reshape(half, 2, GROUP, p * LANES)

        follow(k, n // 2, n - 1)

        def one(s, which):
            x = wide_f[s].reshape(2 * n2, p * LANES)
            z = jnp.dot(mid[which], x, preferred_element_type=F32)
            spec_f[s] = z.reshape(2, n2, p * LANES)

        one(0, 0)

        @pl.loop(1, half, unroll=5)
        def _(s):
            one(s, 1)

    def slabs(k, ss, which):
        x = jnp.concatenate([spec[s].reshape(2 * n2, LANES) for s in ss], 1)
        z = jnp.dot(mid[which], x, preferred_element_type=F32)
        ys = []
        for j, s in enumerate(ss):
            zr = z[:n2, j * LANES : (j + 1) * LANES]
            zi = z[n2:, j * LANES : (j + 1) * LANES]
            rr = ii = cross = None
            for b in range(p):
                xr = zr if b == 0 else pltpu.roll(zr, b * lc, 1)
                xi = zi if b == 0 else pltpu.roll(zi, b * lc, 1)
                gr = spec_f[s, 0, :, b * LANES : (b + 1) * LANES]
                gi = spec_f[s, 1, :, b * LANES : (b + 1) * LANES]
                add = lambda t, v: v if t is None else t + v
                rr = add(rr, xr * gr)
                ii = add(ii, xi * gi)
                cross = add(cross, xr * gi + xi * gr)
            if which == 0:
                top = lax.broadcasted_iota(jnp.int32, (n2, LANES), 0) == 0
                yr = jnp.where(top, rr, rr - ii)
                yi = jnp.where(top, ii, cross)
            else:
                yr, yi = rr - ii, cross
            ys.append(jnp.concatenate((yr, yi), 0).astype(BF16))
        v = jnp.dot(back[which], jnp.concatenate(ys, 1), preferred_element_type=F32)
        for j, s in enumerate(ss):
            spec[s] = v[:, j * LANES : (j + 1) * LANES].astype(BF16).reshape(2, n2, LANES)

    def convolve(k):
        @pl.loop(1, n)
        def _(i):
            send_drive(k, i).wait_recv()

        @pl.loop(0, groups, unroll=groups)
        def _(g):
            x = jnp.concatenate([recv[k, group_rows(g, a), :] for a in range(half)], 0)
            res = jnp.dot(first[g], x, preferred_element_type=F32)
            spec[:, :, group_rows(g), :] = res.astype(BF16).reshape(half, 2, GROUP, LANES)

        slabs(k, [0], 0)
        slabs(k, [1], 1)

        @pl.loop(1, half // 2, unroll=half // 2 - 1)
        def _(t):
            slabs(k, [2 * t, 2 * t + 1], 1)

        direct = jnp.concatenate([skip[:, k * lc : (k + 1) * lc]] * p, 1)

        @pl.loop(0, groups, unroll=groups)
        def _(g):
            v = spec[:, :, group_rows(g), :].reshape(2 * half * GROUP, LANES)
            y = jnp.dot(last[g], v, preferred_element_type=F32)
            for a in range(half):
                at = group_rows(g, a)
                both = y[a * GROUP : (a + 1) * GROUP] + direct * recv[k, at, :].astype(F32)
                done[k, at, :] = both.astype(BF16)

        ret[k, me] = done[k, block_rows(me), :]

        @pl.loop(0, n - 1)
        def _(step):
            send_long(k, offset(step)).start()

    for k in range(chunks):
        filter_spectrum(k)
        convolve(k)

    @pl.when(me < n - 1)
    def _():
        m_copy.wait_send()

    @pl.loop(1, n)
    def _(i):
        send_drive(chunks - 1, i).wait_send()

    @pl.loop(0, tiles)
    def _(step):
        tile = lax.rem(me // own + tiles // 2 + tiles - step, tiles)
        for d in range(own):
            src = tile * own + d

            @pl.when(src != me)
            def _():
                for k in range(chunks):
                    send_long(k, lax.rem(me - src + n, n)).wait_recv()

        parts = [ret[d % chunks, tile * own + d // chunks].astype(F32) for d in range(p)]
        for h in range(p):
            block = None
            for d in range(p):
                shift = ((d - h) % p) * lc
                moved = parts[d] if shift == 0 else pltpu.roll(parts[d], shift, 1)
                block = moved if block is None else jnp.where(lane == d, moved, block)
            drive[tile, pl.ds(h, rpd, stride=p), :] = block
        out[:, lanes_of(tile)] = (query[tile] * drive[tile]).astype(BF16)

    for k in range(chunks):

        @pl.loop(1, n)
        def _(i):
            send_long(k, i).wait_send()


def body(n, projected, taps, filters, skip):
    rows, _, chans = projected.shape
    lc, length = filters.shape
    chunks, sc, p = plan(chans, lc, n)
    rpd = rows // p
    total = length // p
    n1, n2 = factors(2 * total)
    half = n1 // 2
    tables = [jnp.asarray(t) for t in dft_tables(2 * total)]
    vmem = pl.BlockSpec(memory_space=pltpu.VMEM)
    hbm = pl.BlockSpec(memory_space=pl.ANY)
    sems = pltpu.SemaphoreType.DMA((chunks, n))
    blocks = pltpu.VMEM((chunks, n, rpd, LANES), BF16)
    flat = pltpu.VMEM((chunks, total, LANES), BF16)
    moved = jnp.transpose(projected, (1, 0, 2))
    return pl.pallas_call(
        functools.partial(kernel, n, chunks),
        out_shape=jax.ShapeDtypeStruct((rows, chans), BF16),
        in_specs=[hbm, vmem, hbm, vmem] + [hbm] * 4,
        out_specs=vmem,
        scratch_shapes=[
            pltpu.VMEM(moved.shape, BF16),
            pltpu.VMEM((filters.shape[0], LANES + length), BF16),
            *[pltpu.VMEM(t.shape, BF16) for t in tables],
            pltpu.VMEM((3, 16, chans), BF16),
            pltpu.VMEM((chans // LANES, rows, LANES), F32),
            pltpu.VMEM((chans // LANES, rows, LANES), F32),
            blocks,
            flat,
            pltpu.VMEM((chunks, p, total, LANES), BF16),
            pltpu.VMEM((half, 2, n2, p * LANES), BF16),
            pltpu.VMEM((half, 2, n2, p * LANES), F32),
            pltpu.VMEM((half, 2, n2, LANES), BF16),
            flat,
            blocks,
            pltpu.SemaphoreType.DMA((6,)),
            pltpu.SemaphoreType.DMA,
            pltpu.SemaphoreType.DMA,
            sems, sems, sems, sems,
        ],
        compiler_params=pltpu.CompilerParams(
            collective_id=0, has_side_effects=True, vmem_limit_bytes=56 * 1024 * 1024
        ),
    )(moved, taps, filters, skip.reshape(1, lc), *tables)


def solution(mesh):
    placed = (P(("grp", "seq"), None, None), P(), P("seq", None), P("seq"))
    return jax.shard_map(
        functools.partial(body, mesh.shape["seq"]),
        mesh=mesh, in_specs=placed, out_specs=P(("grp", "seq"), None), check_vma=False,
    )
```

```python
import functools
import math

import jax
import jax.numpy as jnp
import numpy as np
from jax import lax
from jax.experimental import pallas as pl
from jax.experimental.pallas import tpu as pltpu
from jax.sharding import PartitionSpec as P

LANES = 128
SUB = 8
GROUP = 16
MAX_PHASES = 4
F32 = jnp.float32
BF16 = jnp.bfloat16


def factors(order):
    inner = 1 << ((int(math.log2(order)) + 1) // 2)
    return order // inner, inner


def dft_tables(order):
    n1, n2 = factors(order)
    half, hb = n1 // 2, n2 // 2
    groups = n2 // GROUP
    s = np.arange(half)[:, None, None]
    a = np.arange(half)[None, :, None]
    b = np.arange(n2)[None, None, :]
    theta = 2 * np.pi * ((s * (a * n2 + b)) % order) / order
    sign = np.broadcast_to((-1.0) ** np.arange(half)[:, None], (half, n2))
    fwd = np.stack((np.cos(theta), -np.sin(theta)), 1)
    fwd[0, 0] = 1.0
    fwd[0, 1] = sign
    inv = np.stack((2 * np.cos(theta), -2 * np.sin(theta)), 1)
    inv[0, 0] = 1.0
    inv[0, 1] = sign
    inv = inv / order
    eye = np.eye(GROUP)
    fwd_g = fwd.reshape(half, 2, half, groups, GROUP)
    first = np.einsum("srage,ef->gsreaf", fwd_g, eye).reshape(groups, 2 * half * GROUP, half * GROUP)
    inv_g = inv.reshape(half, 2, half, groups, GROUP)
    last = np.einsum("srage,ef->gaesrf", inv_g, eye).reshape(groups, half * GROUP, 2 * half * GROUP)
    k = np.arange(n2)
    phi = 2 * np.pi * (np.outer(k, k) % n2) / n2
    c, d = np.cos(phi), np.sin(phi)
    mid = np.block([[c, d], [-d, c]])
    back = np.block([[c, -d], [d, c]])
    kh = np.arange(hb)
    low = 2 * np.pi * (np.outer(kh, k) % n2) / n2
    odd = 2 * np.pi * (np.outer(half + n1 * kh, k) % order) / order
    mid0 = np.zeros((2 * n2, 2 * n2))
    mid0[:hb, :n2] = np.cos(low)
    mid0[hb:n2, n2:] = np.cos(odd)
    mid0[n2 : n2 + hb, :n2] = -np.sin(low)
    mid0[n2, :n2] = (-1.0) ** k
    mid0[n2 + hb :, n2:] = -np.sin(odd)
    back0 = 2 * mid0.T
    back0[:, 0] /= 2
    back0[:, n2] /= 2
    cast = lambda x: np.ascontiguousarray(x.astype(BF16))
    return cast(first), cast(np.stack((mid0, mid))), cast(np.stack((back0, back))), cast(last)


def plan(chans, lc, n):
    chunks = max(1, MAX_PHASES * lc // LANES)
    lc = lc // chunks
    return chunks, lc, LANES // lc


def kernel(
    n, chunks,
    proj_hbm, taps, filt_hbm, skip, first_hbm, mid_hbm, back_hbm, last_hbm,
    out,
    proj, filt, first, mid, back, last,
    margin, query, drive, pack, recv, tok, wide_f, spec_f, spec, done, ret,
    load, m_send, m_recv, send1, recv1, send2, recv2,
):
    me = lax.axis_index("seq")
    _, rows, chans = proj.shape
    count = taps.shape[0]
    lc = chans // n // chunks
    p = LANES // lc
    rpd = rows // p
    total = rpd * n
    n1, n2 = factors(2 * total)
    half = n1 // 2
    groups = n2 // GROUP
    tiles = chans // LANES
    own = p // chunks
    mrows = margin.shape[1]
    lane = lax.broadcasted_iota(jnp.int32, (1, LANES), 1) // lc

    loads = [
        pltpu.make_async_copy(a, b, load.at[k])
        for k, (a, b) in enumerate(
            ((proj_hbm, proj), (filt_hbm, filt.at[:, pl.ds(LANES, total * p)]), (first_hbm, first), (mid_hbm, mid), (back_hbm, back), (last_hbm, last))
        )
    ]
    for c in loads:
        c.start()

    barrier = pltpu.get_barrier_semaphore()

    @pl.loop(1, n)
    def _(i):
        pl.semaphore_signal(barrier, inc=1, device_id={"seq": lax.rem(me + i, n)})

    def lanes_of(tile):
        return pl.ds(pl.multiple_of(tile * LANES, LANES), LANES)

    def features(tile, ext, many):
        feats = []
        for m in range(3):
            x = ext(m)
            from_row = x.shape[0] - many
            acc = None
            for o in range(count):
                term = taps[o, m : m + 1, lanes_of(tile)] * x[from_row - o : from_row - o + many]
                acc = term if acc is None else acc + term
            feats.append(acc)
        return feats[0], (feats[1] * feats[2]).astype(BF16).astype(F32)

    def tile_at(step):
        return lax.rem(me // own + tiles // 2 + step, tiles)

    def tile_features(step):
        tile = tile_at(step)
        zero = jnp.zeros((SUB, LANES), F32)
        q, d = features(
            tile, lambda m: jnp.concatenate((zero, proj[m, :, lanes_of(tile)].astype(F32)), 0), rows
        )
        query[tile] = q
        drive[tile] = d

    pl.semaphore_wait(barrier, n - 1)
    m_copy = pltpu.make_async_remote_copy(
        src_ref=proj_hbm.at[:, pl.ds(rows - mrows, mrows)],
        dst_ref=margin,
        send_sem=m_send,
        recv_sem=m_recv,
        device_id={"seq": lax.rem(me + 1, n)},
    )

    @pl.when(me < n - 1)
    def _():
        m_copy.start()

    loads[0].wait()
    early = tiles // 2
    pl.loop(0, early, unroll=2)(tile_features)

    @pl.when(me > 0)
    def _():
        m_copy.wait_recv()

    @pl.when(me == 0)
    def _():
        margin[...] = jnp.zeros_like(margin)

    def block_rows(j):
        return pl.ds(pl.multiple_of(j * rpd, GROUP), rpd)

    def send_drive(k, i):
        dest = lax.rem(me + i, n)
        return pltpu.make_async_remote_copy(
            src_ref=pack.at[k, dest],
            dst_ref=recv.at[k, block_rows(me)],
            send_sem=send1.at[k, i],
            recv_sem=recv1.at[k, i],
            device_id={"seq": dest},
        )

    def send_long(k, i):
        dest = lax.rem(me + i, n)
        return pltpu.make_async_remote_copy(
            src_ref=done.at[k, block_rows(dest)],
            dst_ref=ret.at[k, me],
            send_sem=send2.at[k, i],
            recv_sem=recv2.at[k, i],
            device_id={"seq": dest},
        )

    def send_tile(step):
        tile = tile_at(step)

        def ext(m):
            before = margin[m, :, lanes_of(tile)].astype(F32)
            after = proj[m, 0:16, lanes_of(tile)].astype(F32)
            return jnp.concatenate((before[mrows - SUB :], after[:SUB]), 0)

        q, dr = features(tile, ext, SUB)
        query[tile, 0:SUB] = q
        drive[tile, 0:SUB] = dr
        parts = [drive[tile, pl.ds(h, rpd, stride=p), :] for h in range(p)]
        for d in range(p):
            block = None
            for h in range(p):
                shift = ((h - d) % p) * lc
                moved = parts[h] if shift == 0 else pltpu.roll(parts[h], shift, 1)
                block = moved if block is None else jnp.where(lane == h, moved, block)
            block = block.astype(BF16)
            dest, k = tile * own + d // chunks, d % chunks

            @pl.when(dest == me)
            def _():
                recv[k, block_rows(me), :] = block

            @pl.when(dest != me)
            def _():
                pack[k, dest] = block
                if k == 0:
                    send_drive(k, lax.rem(dest - me + n, n)).start()

    pl.loop(0, early, unroll=2)(send_tile)

    @pl.loop(early, tiles)
    def _(step):
        tile_features(step)
        send_tile(step)

    def offset(step):
        return lax.rem(n // 2 + step, n - 1) + 1

    def follow(k, lo, hi):
        if k + 1 < chunks:

            @pl.loop(lo, hi)
            def _(step):
                send_drive(k, offset(step)).wait_send()
                send_drive(k + 1, offset(step)).start()

    loads[1].wait()
    seg = LANES // p
    row_id = lax.broadcasted_iota(jnp.int32, (2 * LANES, 2 * LANES), 0)
    col_id = lax.broadcasted_iota(jnp.int32, (2 * LANES, 2 * LANES), 1)
    inside = lax.rem(row_id, LANES)
    source = LANES + p * lax.rem(inside, seg) + inside // seg - jnp.where(row_id < LANES, 0, p)
    apart = (col_id == source).astype(F32).astype(BF16)
    filt[:, 0:LANES] = jnp.zeros((filt.shape[0], LANES), BF16)

    @pl.loop(0, total // seg, unroll=4)
    def _(t):
        piece = filt[:, pl.ds(pl.multiple_of(t * LANES, LANES), 2 * LANES)]
        wide = jnp.concatenate([piece[k * lc : (k + 1) * lc] for k in range(chunks) for _ in range(p)], 0)
        turned = lax.dot_general(apart, wide, (((1,), (1,)), ((), ())), preferred_element_type=F32)
        at = pl.ds(pl.multiple_of(t * seg, GROUP), seg)
        for k in range(chunks):
            for b in range(p):
                now = turned[b * seg : (b + 1) * seg, k * LANES : (k + 1) * LANES]
                old = turned[LANES + b * seg : LANES + (b + 1) * seg, k * LANES : (k + 1) * LANES]
                tok[k, b, at, :] = jnp.where(lane < b, old, now).astype(BF16)

    for c in loads[2:]:
        c.wait()

    def group_rows(g, a=0):
        return pl.ds(pl.multiple_of(a * n2 + GROUP * g, GROUP), GROUP)

    def filter_first(k):
        @pl.loop(0, groups, unroll=2)
        def _(g):
            wide = jnp.concatenate(
                [
                    jnp.concatenate([tok[k, b, group_rows(g, a), :] for a in range(half)], 0)
                    for b in range(p)
                ],
                1,
            )
            res = jnp.dot(first[g], wide, preferred_element_type=F32)
            wide_f[:, :, group_rows(g), :] = res.astype(BF16).reshape(half, 2, GROUP, p * LANES)

    def filter_last(k):
        def one(s, which):
            x = wide_f[s].reshape(2 * n2, p * LANES)
            z = jnp.dot(mid[which], x, preferred_element_type=F32)
            spec_f[s] = z.reshape(2, n2, p * LANES)

        one(0, 0)

        @pl.loop(1, half, unroll=5)
        def _(s):
            one(s, 1)

    def slabs(k, ss, which):
        x = jnp.concatenate([spec[s].reshape(2 * n2, LANES) for s in ss], 1)
        z = jnp.dot(mid[which], x, preferred_element_type=F32)
        ys = []
        for j, s in enumerate(ss):
            zr = z[:n2, j * LANES : (j + 1) * LANES]
            zi = z[n2:, j * LANES : (j + 1) * LANES]
            rr = ii = cross = None
            for b in range(p):
                xr = zr if b == 0 else pltpu.roll(zr, b * lc, 1)
                xi = zi if b == 0 else pltpu.roll(zi, b * lc, 1)
                gr = spec_f[s, 0, :, b * LANES : (b + 1) * LANES]
                gi = spec_f[s, 1, :, b * LANES : (b + 1) * LANES]
                add = lambda t, v: v if t is None else t + v
                rr = add(rr, xr * gr)
                ii = add(ii, xi * gi)
                cross = add(cross, xr * gi + xi * gr)
            if which == 0:
                top = lax.broadcasted_iota(jnp.int32, (n2, LANES), 0) == 0
                yr = jnp.where(top, rr, rr - ii)
                yi = jnp.where(top, ii, cross)
            else:
                yr, yi = rr - ii, cross
            ys.append(jnp.concatenate((yr, yi), 0).astype(BF16))
        v = jnp.dot(back[which], jnp.concatenate(ys, 1), preferred_element_type=F32)
        for j, s in enumerate(ss):
            spec[s] = v[:, j * LANES : (j + 1) * LANES].astype(BF16).reshape(2, n2, LANES)

    def convolve(k):
        @pl.loop(1, n)
        def _(i):
            send_drive(k, i).wait_recv()

        @pl.loop(0, groups, unroll=groups)
        def _(g):
            x = jnp.concatenate([recv[k, group_rows(g, a), :] for a in range(half)], 0)
            res = jnp.dot(first[g], x, preferred_element_type=F32)
            spec[:, :, group_rows(g), :] = res.astype(BF16).reshape(half, 2, GROUP, LANES)

        slabs(k, [0], 0)
        slabs(k, [1], 1)

        @pl.loop(1, half // 2, unroll=half // 2 - 1)
        def _(t):
            slabs(k, [2 * t, 2 * t + 1], 1)

        direct = jnp.concatenate([skip[:, k * lc : (k + 1) * lc]] * p, 1)

        @pl.loop(0, groups, unroll=groups)
        def _(g):
            v = spec[:, :, group_rows(g), :].reshape(2 * half * GROUP, LANES)
            y = jnp.dot(last[g], v, preferred_element_type=F32)
            for a in range(half):
                at = group_rows(g, a)
                both = y[a * GROUP : (a + 1) * GROUP] + direct * recv[k, at, :].astype(F32)
                done[k, at, :] = both.astype(BF16)

        ret[k, me] = done[k, block_rows(me), :]

        @pl.loop(0, n - 1)
        def _(step):
            send_long(k, offset(step)).start()

    filter_first(0)
    for k in range(chunks):
        follow(k, 0, n // 2)
        filter_last(k)
        follow(k, n // 2, n - 1)
        if k + 1 < chunks:
            filter_first(k + 1)
        convolve(k)

    @pl.when(me < n - 1)
    def _():
        m_copy.wait_send()

    @pl.loop(1, n)
    def _(i):
        send_drive(chunks - 1, i).wait_send()

    @pl.loop(0, tiles)
    def _(step):
        tile = lax.rem(me // own + tiles // 2 + tiles - step, tiles)
        for d in range(own):
            src = tile * own + d

            @pl.when(src != me)
            def _():
                for k in range(chunks):
                    send_long(k, lax.rem(me - src + n, n)).wait_recv()

        parts = [ret[d % chunks, tile * own + d // chunks].astype(F32) for d in range(p)]
        for h in range(p):
            block = None
            for d in range(p):
                shift = ((d - h) % p) * lc
                moved = parts[d] if shift == 0 else pltpu.roll(parts[d], shift, 1)
                block = moved if block is None else jnp.where(lane == d, moved, block)
            drive[tile, pl.ds(h, rpd, stride=p), :] = block
        out[:, lanes_of(tile)] = (query[tile] * drive[tile]).astype(BF16)

    for k in range(chunks):

        @pl.loop(1, n)
        def _(i):
            send_long(k, i).wait_send()


def body(n, projected, taps, filters, skip):
    rows, _, chans = projected.shape
    lc, length = filters.shape
    chunks, sc, p = plan(chans, lc, n)
    rpd = rows // p
    total = length // p
    n1, n2 = factors(2 * total)
    half = n1 // 2
    tables = [jnp.asarray(t) for t in dft_tables(2 * total)]
    vmem = pl.BlockSpec(memory_space=pltpu.VMEM)
    hbm = pl.BlockSpec(memory_space=pl.ANY)
    sems = pltpu.SemaphoreType.DMA((chunks, n))
    blocks = pltpu.VMEM((chunks, n, rpd, LANES), BF16)
    flat = pltpu.VMEM((chunks, total, LANES), BF16)
    moved = jnp.transpose(projected, (1, 0, 2))
    return pl.pallas_call(
        functools.partial(kernel, n, chunks),
        out_shape=jax.ShapeDtypeStruct((rows, chans), BF16),
        in_specs=[hbm, vmem, hbm, vmem] + [hbm] * 4,
        out_specs=vmem,
        scratch_shapes=[
            pltpu.VMEM(moved.shape, BF16),
            pltpu.VMEM((filters.shape[0], LANES + length), BF16),
            *[pltpu.VMEM(t.shape, BF16) for t in tables],
            pltpu.VMEM((3, 16, chans), BF16),
            pltpu.VMEM((chans // LANES, rows, LANES), F32),
            pltpu.VMEM((chans // LANES, rows, LANES), F32),
            blocks,
            flat,
            pltpu.VMEM((chunks, p, total, LANES), BF16),
            pltpu.VMEM((half, 2, n2, p * LANES), BF16),
            pltpu.VMEM((half, 2, n2, p * LANES), F32),
            pltpu.VMEM((half, 2, n2, LANES), BF16),
            flat,
            blocks,
            pltpu.SemaphoreType.DMA((6,)),
            pltpu.SemaphoreType.DMA,
            pltpu.SemaphoreType.DMA,
            sems, sems, sems, sems,
        ],
        compiler_params=pltpu.CompilerParams(
            collective_id=0, has_side_effects=True, vmem_limit_bytes=56 * 1024 * 1024
        ),
    )(moved, taps, filters, skip.reshape(1, lc), *tables)


def solution(mesh):
    placed = (P(("grp", "seq"), None, None), P(), P("seq", None), P("seq"))
    return jax.shard_map(
        functools.partial(body, mesh.shape["seq"]),
        mesh=mesh, in_specs=placed, out_specs=P(("grp", "seq"), None), check_vma=False,
    )
```

```python
import functools
import math

import jax
import jax.numpy as jnp
import numpy as np
from jax import lax
from jax.experimental import pallas as pl
from jax.experimental.pallas import tpu as pltpu
from jax.sharding import PartitionSpec as P

LANES = 128
SUB = 8
GROUP = 16
MAX_PHASES = 4
ROOM = 6 * 1024 * 1024
F32 = jnp.float32
BF16 = jnp.bfloat16


def factors(order):
    inner = 1 << ((int(math.log2(order)) + 1) // 2)
    return order // inner, inner


def dft_tables(order):
    n1, n2 = factors(order)
    half, hb = n1 // 2, n2 // 2
    groups = n2 // GROUP
    s = np.arange(half)[:, None, None]
    a = np.arange(half)[None, :, None]
    b = np.arange(n2)[None, None, :]
    theta = 2 * np.pi * ((s * (a * n2 + b)) % order) / order
    sign = np.broadcast_to((-1.0) ** np.arange(half)[:, None], (half, n2))
    fwd = np.stack((np.cos(theta), -np.sin(theta)), 1)
    fwd[0, 0] = 1.0
    fwd[0, 1] = sign
    inv = np.stack((2 * np.cos(theta), -2 * np.sin(theta)), 1)
    inv[0, 0] = 1.0
    inv[0, 1] = sign
    inv = inv / order
    eye = np.eye(GROUP)
    fwd_g = fwd.reshape(half, 2, half, groups, GROUP)
    first = np.einsum("srage,ef->gsreaf", fwd_g, eye).reshape(groups, 2 * half * GROUP, half * GROUP)
    inv_g = inv.reshape(half, 2, half, groups, GROUP)
    last = np.einsum("srage,ef->gaesrf", inv_g, eye).reshape(groups, half * GROUP, 2 * half * GROUP)
    k = np.arange(n2)
    phi = 2 * np.pi * (np.outer(k, k) % n2) / n2
    c, d = np.cos(phi), np.sin(phi)
    mid = np.block([[c, d], [-d, c]])
    back = np.block([[c, -d], [d, c]])
    kh = np.arange(hb)
    low = 2 * np.pi * (np.outer(kh, k) % n2) / n2
    odd = 2 * np.pi * (np.outer(half + n1 * kh, k) % order) / order
    mid0 = np.zeros((2 * n2, 2 * n2))
    mid0[:hb, :n2] = np.cos(low)
    mid0[hb:n2, n2:] = np.cos(odd)
    mid0[n2 : n2 + hb, :n2] = -np.sin(low)
    mid0[n2, :n2] = (-1.0) ** k
    mid0[n2 + hb :, n2:] = -np.sin(odd)
    back0 = 2 * mid0.T
    back0[:, 0] /= 2
    back0[:, n2] /= 2
    cast = lambda x: np.ascontiguousarray(x.astype(BF16))
    return cast(first), cast(np.stack((mid0, mid))), cast(np.stack((back0, back))), cast(last)


def plan(chans, lc, n):
    chunks = max(1, MAX_PHASES * lc // LANES)
    lc = lc // chunks
    return chunks, lc, LANES // lc


def kernel(
    n, chunks,
    proj_hbm, taps, filt_hbm, skip, first_hbm, mid_hbm, back_hbm, last_hbm,
    out,
    proj, filt, first, mid, back, last,
    margin, query, drive, pack, recv, tok, wide_f, spec_f, spec, done, ret,
    load, m_send, m_recv, send1, recv1, send2, recv2,
):
    me = lax.axis_index("seq")
    _, rows, chans = proj.shape
    count = taps.shape[0]
    lc = chans // n // chunks
    p = LANES // lc
    rpd = rows // p
    total = rpd * n
    n1, n2 = factors(2 * total)
    half = n1 // 2
    groups = n2 // GROUP
    tiles = chans // LANES
    own = p // chunks
    mrows = margin.shape[1]
    lane = lax.broadcasted_iota(jnp.int32, (1, LANES), 1) // lc

    loads = [
        pltpu.make_async_copy(a, b, load.at[k])
        for k, (a, b) in enumerate(
            ((proj_hbm, proj), (filt_hbm, filt.at[:, pl.ds(LANES, total * p)]), (first_hbm, first), (mid_hbm, mid), (back_hbm, back), (last_hbm, last))
        )
    ]
    for c in loads:
        c.start()

    barrier = pltpu.get_barrier_semaphore()

    @pl.loop(1, n)
    def _(i):
        pl.semaphore_signal(barrier, inc=1, device_id={"seq": lax.rem(me + i, n)})

    def lanes_of(tile):
        return pl.ds(pl.multiple_of(tile * LANES, LANES), LANES)

    def features(tile, ext, many):
        feats = []
        for m in range(3):
            x = ext(m)
            from_row = x.shape[0] - many
            acc = None
            for o in range(count):
                term = taps[o, m : m + 1, lanes_of(tile)] * x[from_row - o : from_row - o + many]
                acc = term if acc is None else acc + term
            feats.append(acc)
        return feats[0], (feats[1] * feats[2]).astype(BF16).astype(F32)

    def tile_at(step):
        return lax.rem(me // own + tiles // 2 + step, tiles)

    def tile_features(step):
        tile = tile_at(step)
        zero = jnp.zeros((SUB, LANES), F32)
        q, d = features(
            tile, lambda m: jnp.concatenate((zero, proj[m, :, lanes_of(tile)].astype(F32)), 0), rows
        )
        query[tile] = q
        drive[tile] = d

    loads[0].wait()
    pl.loop(0, tiles // 2)(tile_features)

    pl.semaphore_wait(barrier, n - 1)
    m_copy = pltpu.make_async_remote_copy(
        src_ref=proj.at[:, pl.ds(rows - mrows, mrows)],
        dst_ref=margin,
        send_sem=m_send,
        recv_sem=m_recv,
        device_id={"seq": lax.rem(me + 1, n)},
    )

    @pl.when(me < n - 1)
    def _():
        m_copy.start()

    early = 3 * tiles // 4
    pl.loop(tiles // 2, early)(tile_features)

    @pl.when(me > 0)
    def _():
        m_copy.wait_recv()

    @pl.when(me == 0)
    def _():
        margin[...] = jnp.zeros_like(margin)

    def block_rows(j):
        return pl.ds(pl.multiple_of(j * rpd, GROUP), rpd)

    def send_drive(k, i):
        dest = lax.rem(me + i, n)
        return pltpu.make_async_remote_copy(
            src_ref=pack.at[k, dest],
            dst_ref=recv.at[k, block_rows(me)],
            send_sem=send1.at[k, i],
            recv_sem=recv1.at[k, i],
            device_id={"seq": dest},
        )

    def send_long(k, i):
        dest = lax.rem(me + i, n)
        return pltpu.make_async_remote_copy(
            src_ref=done.at[k, block_rows(dest)],
            dst_ref=ret.at[k, me],
            send_sem=send2.at[k, i],
            recv_sem=recv2.at[k, i],
            device_id={"seq": dest},
        )

    def send_tile(step):
        tile = tile_at(step)

        def ext(m):
            before = margin[m, :, lanes_of(tile)].astype(F32)
            after = proj[m, 0:16, lanes_of(tile)].astype(F32)
            return jnp.concatenate((before[mrows - SUB :], after[:SUB]), 0)

        q, dr = features(tile, ext, SUB)
        query[tile, 0:SUB] = q
        drive[tile, 0:SUB] = dr
        parts = [drive[tile, pl.ds(h, rpd, stride=p), :] for h in range(p)]
        for d in range(p):
            block = None
            for h in range(p):
                shift = ((h - d) % p) * lc
                moved = parts[h] if shift == 0 else pltpu.roll(parts[h], shift, 1)
                block = moved if block is None else jnp.where(lane == h, moved, block)
            block = block.astype(BF16)
            dest, k = tile * own + d // chunks, d % chunks

            @pl.when(dest == me)
            def _():
                recv[k, block_rows(me), :] = block

            @pl.when(dest != me)
            def _():
                pack[k, dest] = block
                if k == 0:
                    send_drive(k, lax.rem(dest - me + n, n)).start()

    pl.loop(0, early, unroll=2)(send_tile)

    @pl.loop(early, tiles)
    def _(step):
        tile_features(step)
        send_tile(step)

    def offset(step):
        return lax.rem(n // 2 + step, n - 1) + 1

    def follow(k, lo, hi):
        if k + 1 < chunks:

            @pl.loop(lo, hi)
            def _(step):
                send_drive(k, offset(step)).wait_send()
                send_drive(k + 1, offset(step)).start()

    loads[1].wait()
    seg = LANES // p
    row_id = lax.broadcasted_iota(jnp.int32, (2 * LANES, 2 * LANES), 0)
    col_id = lax.broadcasted_iota(jnp.int32, (2 * LANES, 2 * LANES), 1)
    inside = lax.rem(row_id, LANES)
    source = LANES + p * lax.rem(inside, seg) + inside // seg - jnp.where(row_id < LANES, 0, p)
    apart = (col_id == source).astype(F32).astype(BF16)
    filt[:, 0:LANES] = jnp.zeros((filt.shape[0], LANES), BF16)

    @pl.loop(0, total // seg, unroll=4)
    def _(t):
        piece = filt[:, pl.ds(pl.multiple_of(t * LANES, LANES), 2 * LANES)]
        wide = jnp.concatenate([piece[k * lc : (k + 1) * lc] for k in range(chunks) for _ in range(p)], 0)
        turned = lax.dot_general(apart, wide, (((1,), (1,)), ((), ())), preferred_element_type=F32)
        at = pl.ds(pl.multiple_of(t * seg, GROUP), seg)
        for k in range(chunks):
            for b in range(p):
                now = turned[b * seg : (b + 1) * seg, k * LANES : (k + 1) * LANES]
                old = turned[LANES + b * seg : LANES + (b + 1) * seg, k * LANES : (k + 1) * LANES]
                tok[k, b, at, :] = jnp.where(lane < b, old, now).astype(BF16)

    for c in loads[2:]:
        c.wait()

    def group_rows(g, a=0):
        return pl.ds(pl.multiple_of(a * n2 + GROUP * g, GROUP), GROUP)

    def filter_spectrum(k):
        follow(k, 0, n // 2)

        @pl.loop(0, groups, unroll=2)
        def _(g):
            wide = jnp.concatenate(
                [
                    jnp.concatenate([tok[k, b, group_rows(g, a), :] for a in range(half)], 0)
                    for b in range(p)
                ],
                1,
            )
            res = jnp.dot(first[g], wide, preferred_element_type=F32)
            wide_f[:, :, group_rows(g), :] = res.astype(BF16).reshape(half, 2, GROUP, p * LANES)

        follow(k, n // 2, n - 1)

        def one(s, which):
            x = wide_f[s].reshape(2 * n2, p * LANES)
            z = jnp.dot(mid[which], x, preferred_element_type=F32)
            spec_f[s] = z.reshape(2, n2, p * LANES)

        one(0, 0)

        @pl.loop(1, half, unroll=5)
        def _(s):
            one(s, 1)

    def slabs(k, ss, which):
        x = jnp.concatenate([spec[s].reshape(2 * n2, LANES) for s in ss], 1)
        z = jnp.dot(mid[which], x, preferred_element_type=F32)
        ys = []
        for j, s in enumerate(ss):
            zr = z[:n2, j * LANES : (j + 1) * LANES]
            zi = z[n2:, j * LANES : (j + 1) * LANES]
            rr = ii = cross = None
            for b in range(p):
                xr = zr if b == 0 else pltpu.roll(zr, b * lc, 1)
                xi = zi if b == 0 else pltpu.roll(zi, b * lc, 1)
                gr = spec_f[s, 0, :, b * LANES : (b + 1) * LANES]
                gi = spec_f[s, 1, :, b * LANES : (b + 1) * LANES]
                add = lambda t, v: v if t is None else t + v
                rr = add(rr, xr * gr)
                ii = add(ii, xi * gi)
                cross = add(cross, xr * gi + xi * gr)
            if which == 0:
                top = lax.broadcasted_iota(jnp.int32, (n2, LANES), 0) == 0
                yr = jnp.where(top, rr, rr - ii)
                yi = jnp.where(top, ii, cross)
            else:
                yr, yi = rr - ii, cross
            ys.append(jnp.concatenate((yr, yi), 0).astype(BF16))
        v = jnp.dot(back[which], jnp.concatenate(ys, 1), preferred_element_type=F32)
        for j, s in enumerate(ss):
            spec[s] = v[:, j * LANES : (j + 1) * LANES].astype(BF16).reshape(2, n2, LANES)

    def convolve(k):
        @pl.loop(1, n)
        def _(i):
            send_drive(k, i).wait_recv()

        @pl.loop(0, groups, unroll=groups)
        def _(g):
            x = jnp.concatenate([recv[k, group_rows(g, a), :] for a in range(half)], 0)
            res = jnp.dot(first[g], x, preferred_element_type=F32)
            spec[:, :, group_rows(g), :] = res.astype(BF16).reshape(half, 2, GROUP, LANES)

        slabs(k, [0], 0)
        slabs(k, [1], 1)

        @pl.loop(1, half // 2, unroll=half // 2 - 1)
        def _(t):
            slabs(k, [2 * t, 2 * t + 1], 1)

        direct = jnp.concatenate([skip[:, k * lc : (k + 1) * lc]] * p, 1)

        @pl.loop(0, groups, unroll=groups)
        def _(g):
            v = spec[:, :, group_rows(g), :].reshape(2 * half * GROUP, LANES)
            y = jnp.dot(last[g], v, preferred_element_type=F32)
            for a in range(half):
                at = group_rows(g, a)
                both = y[a * GROUP : (a + 1) * GROUP] + direct * recv[k, at, :].astype(F32)
                done[k, at, :] = both.astype(BF16)

        ret[k, me] = done[k, block_rows(me), :]

        @pl.loop(0, n - 1)
        def _(step):
            send_long(k, offset(step)).start()

    for k in range(chunks):
        filter_spectrum(k)
        convolve(k)

    @pl.when(me < n - 1)
    def _():
        m_copy.wait_send()

    @pl.loop(1, n)
    def _(i):
        send_drive(chunks - 1, i).wait_send()

    @pl.loop(0, tiles)
    def _(step):
        tile = lax.rem(me // own + tiles // 2 + tiles - step, tiles)
        for d in range(own):
            src = tile * own + d

            @pl.when(src != me)
            def _():
                for k in range(chunks):
                    send_long(k, lax.rem(me - src + n, n)).wait_recv()

        parts = [ret[d % chunks, tile * own + d // chunks].astype(F32) for d in range(p)]
        for h in range(p):
            block = None
            for d in range(p):
                shift = ((d - h) % p) * lc
                moved = parts[d] if shift == 0 else pltpu.roll(parts[d], shift, 1)
                block = moved if block is None else jnp.where(lane == d, moved, block)
            drive[tile, pl.ds(h, rpd, stride=p), :] = block
        out[:, lanes_of(tile)] = (query[tile] * drive[tile]).astype(BF16)

    for k in range(chunks):

        @pl.loop(1, n)
        def _(i):
            send_long(k, i).wait_send()


def body(n, projected, taps, filters, skip):
    rows, _, chans = projected.shape
    lc, length = filters.shape
    chunks, sc, p = plan(chans, lc, n)
    rpd = rows // p
    total = length // p
    n1, n2 = factors(2 * total)
    half = n1 // 2
    tables = [jnp.asarray(t) for t in dft_tables(2 * total)]
    vmem = pl.BlockSpec(memory_space=pltpu.VMEM)
    hbm = pl.BlockSpec(memory_space=pltpu.HBM)
    sems = pltpu.SemaphoreType.DMA((chunks, n))
    blocks = pltpu.VMEM((chunks, n, rpd, LANES), BF16)
    flat = pltpu.VMEM((chunks, total, LANES), BF16)
    moved = jnp.transpose(projected, (1, 0, 2))
    scratch = [
        pltpu.VMEM(moved.shape, BF16),
        pltpu.VMEM((filters.shape[0], LANES + length), BF16),
        *[pltpu.VMEM(t.shape, BF16) for t in tables],
        pltpu.VMEM((3, 16, chans), BF16),
        pltpu.VMEM((chans // LANES, rows, LANES), F32),
        pltpu.VMEM((chans // LANES, rows, LANES), F32),
        blocks,
        flat,
        pltpu.VMEM((chunks, p, total, LANES), BF16),
        pltpu.VMEM((half, 2, n2, p * LANES), BF16),
        pltpu.VMEM((half, 2, n2, p * LANES), F32),
        pltpu.VMEM((half, 2, n2, LANES), BF16),
        flat,
        blocks,
        pltpu.SemaphoreType.DMA((6,)),
        pltpu.SemaphoreType.DMA,
        pltpu.SemaphoreType.DMA,
        sems, sems, sems, sems,
    ]
    held = sum(math.prod(x.shape) * x.dtype.itemsize for x in scratch if getattr(x, "memory_space", None) == pltpu.VMEM)
    return pl.pallas_call(
        functools.partial(kernel, n, chunks),
        out_shape=jax.ShapeDtypeStruct((rows, chans), BF16),
        in_specs=[hbm, vmem, hbm, vmem] + [hbm] * 4,
        out_specs=vmem,
        scratch_shapes=scratch,
        compiler_params=pltpu.CompilerParams(
            collective_id=0, has_side_effects=True, vmem_limit_bytes=held + ROOM
        ),
    )(moved, taps, filters, skip.reshape(1, lc), *tables)


def solution(mesh):
    placed = (P(("grp", "seq"), None, None), P(), P("seq", None), P("seq"))
    return jax.shard_map(
        functools.partial(body, mesh.shape["seq"]),
        mesh=mesh, in_specs=placed, out_specs=P(("grp", "seq"), None), check_vma=False,
    )
```

```python
import functools
import math

import jax
import jax.numpy as jnp
import numpy as np
from jax import lax
from jax.experimental import pallas as pl
from jax.experimental.pallas import tpu as pltpu
from jax.sharding import PartitionSpec as P

LANES = 128
SUB = 8
GROUP = 16
MAX_PHASES = 4
F32 = jnp.float32
BF16 = jnp.bfloat16


def factors(order):
    inner = 1 << ((int(math.log2(order)) + 1) // 2)
    return order // inner, inner


def dft_tables(order):
    n1, n2 = factors(order)
    half, hb = n1 // 2, n2 // 2
    groups = n2 // GROUP
    s = np.arange(half)[:, None, None]
    a = np.arange(half)[None, :, None]
    b = np.arange(n2)[None, None, :]
    theta = 2 * np.pi * ((s * (a * n2 + b)) % order) / order
    sign = np.broadcast_to((-1.0) ** np.arange(half)[:, None], (half, n2))
    fwd = np.stack((np.cos(theta), -np.sin(theta)), 1)
    fwd[0, 0] = 1.0
    fwd[0, 1] = sign
    inv = np.stack((2 * np.cos(theta), -2 * np.sin(theta)), 1)
    inv[0, 0] = 1.0
    inv[0, 1] = sign
    inv = inv / order
    eye = np.eye(GROUP)
    fwd_g = fwd.reshape(half, 2, half, groups, GROUP)
    first = np.einsum("srage,ef->gsreaf", fwd_g, eye).reshape(groups, 2 * half * GROUP, half * GROUP)
    inv_g = inv.reshape(half, 2, half, groups, GROUP)
    last = np.einsum("srage,ef->gaesrf", inv_g, eye).reshape(groups, half * GROUP, 2 * half * GROUP)
    k = np.arange(n2)
    phi = 2 * np.pi * (np.outer(k, k) % n2) / n2
    c, d = np.cos(phi), np.sin(phi)
    mid = np.block([[c, d], [-d, c]])
    back = np.block([[c, -d], [d, c]])
    kh = np.arange(hb)
    low = 2 * np.pi * (np.outer(kh, k) % n2) / n2
    odd = 2 * np.pi * (np.outer(half + n1 * kh, k) % order) / order
    mid0 = np.zeros((2 * n2, 2 * n2))
    mid0[:hb, :n2] = np.cos(low)
    mid0[hb:n2, n2:] = np.cos(odd)
    mid0[n2 : n2 + hb, :n2] = -np.sin(low)
    mid0[n2, :n2] = (-1.0) ** k
    mid0[n2 + hb :, n2:] = -np.sin(odd)
    back0 = 2 * mid0.T
    back0[:, 0] /= 2
    back0[:, n2] /= 2
    cast = lambda x: np.ascontiguousarray(x.astype(BF16))
    return cast(first), cast(np.stack((mid0, mid))), cast(np.stack((back0, back))), cast(last)


def plan(chans, lc, n):
    chunks = max(1, MAX_PHASES * lc // LANES)
    lc = lc // chunks
    return chunks, lc, LANES // lc


def kernel(
    n, chunks,
    proj_hbm, taps, filt_hbm, skip, first_hbm, mid_hbm, back_hbm, last_hbm,
    out,
    proj, filt, first, mid, back, last,
    margin, query, drive, pack, pack_top, recv, tok, wide_f, spec_f, spec, done, ret,
    load, m_send, m_recv, send1, recv1, send2, recv2, send_t, recv_t,
):
    me = lax.axis_index("seq")
    _, rows, chans = proj.shape
    count = taps.shape[0]
    lc = chans // n // chunks
    p = LANES // lc
    rpd = rows // p
    total = rpd * n
    n1, n2 = factors(2 * total)
    half = n1 // 2
    groups = n2 // GROUP
    tiles = chans // LANES
    own = p // chunks
    mrows = margin.shape[1]
    lane = lax.broadcasted_iota(jnp.int32, (1, LANES), 1) // lc

    loads = [
        pltpu.make_async_copy(a, b, load.at[k])
        for k, (a, b) in enumerate(
            ((proj_hbm, proj), (filt_hbm, filt.at[:, pl.ds(LANES, total * p)]), (first_hbm, first), (mid_hbm, mid), (back_hbm, back), (last_hbm, last))
        )
    ]
    for c in loads:
        c.start()

    barrier = pltpu.get_barrier_semaphore()

    @pl.loop(1, n)
    def _(i):
        pl.semaphore_signal(barrier, inc=1, device_id={"seq": lax.rem(me + i, n)})

    def lanes_of(tile):
        return pl.ds(pl.multiple_of(tile * LANES, LANES), LANES)

    def features(tile, ext, many):
        feats = []
        for m in range(3):
            x = ext(m)
            from_row = x.shape[0] - many
            acc = None
            for o in range(count):
                term = taps[o, m : m + 1, lanes_of(tile)] * x[from_row - o : from_row - o + many]
                acc = term if acc is None else acc + term
            feats.append(acc)
        return feats[0], (feats[1] * feats[2]).astype(BF16).astype(F32)

    def tile_at(step):
        return lax.rem(me // own + tiles // 2 + step, tiles)

    def tile_features(step):
        tile = tile_at(step)
        zero = jnp.zeros((SUB, LANES), F32)
        q, d = features(
            tile, lambda m: jnp.concatenate((zero, proj[m, :, lanes_of(tile)].astype(F32)), 0), rows
        )
        query[tile] = q
        drive[tile] = d

    loads[0].wait()
    early = tiles // 4
    pl.loop(0, early)(tile_features)

    pl.semaphore_wait(barrier, n - 1)
    m_copy = pltpu.make_async_remote_copy(
        src_ref=proj.at[:, pl.ds(rows - mrows, mrows)],
        dst_ref=margin,
        send_sem=m_send,
        recv_sem=m_recv,
        device_id={"seq": lax.rem(me + 1, n)},
    )

    @pl.when(me < n - 1)
    def _():
        m_copy.start()

    def block_rows(j, lo=0, hi=rpd):
        return pl.ds(pl.multiple_of(j * rpd + lo, GROUP), hi - lo)

    def send_drive(k, i):
        dest = lax.rem(me + i, n)
        lo = GROUP if k == 0 else 0
        return pltpu.make_async_remote_copy(
            src_ref=pack.at[k, dest, pl.ds(lo, rpd - lo)],
            dst_ref=recv.at[k, block_rows(me, lo)],
            send_sem=send1.at[k, i],
            recv_sem=recv1.at[k, i],
            device_id={"seq": dest},
        )

    def send_top(i):
        dest = lax.rem(me + i, n)
        return pltpu.make_async_remote_copy(
            src_ref=pack_top.at[dest],
            dst_ref=recv.at[0, block_rows(me, 0, GROUP)],
            send_sem=send_t.at[i],
            recv_sem=recv_t.at[i],
            device_id={"seq": dest},
        )

    def send_long(k, i):
        dest = lax.rem(me + i, n)
        return pltpu.make_async_remote_copy(
            src_ref=done.at[k, block_rows(dest)],
            dst_ref=ret.at[k, me],
            send_sem=send2.at[k, i],
            recv_sem=recv2.at[k, i],
            device_id={"seq": dest},
        )

    def pack_rows(tile, lo, hi):
        parts = [drive[tile, pl.ds(h + p * lo, hi - lo, stride=p), :] for h in range(p)]
        for d in range(p):
            block = None
            for h in range(p):
                shift = ((h - d) % p) * lc
                moved = parts[h] if shift == 0 else pltpu.roll(parts[h], shift, 1)
                block = moved if block is None else jnp.where(lane == h, moved, block)
            block = block.astype(BF16)
            dest, k = tile * own + d // chunks, d % chunks
            top = k == 0 and lo == 0

            @pl.when(dest == me)
            def _():
                recv[k, block_rows(me, lo, hi), :] = block

            @pl.when(dest != me)
            def _():
                if top:
                    pack_top[dest] = block
                    send_top(lax.rem(dest - me + n, n)).start()
                else:
                    pack[k, dest, lo:hi, :] = block
                    if k == 0:
                        send_drive(k, lax.rem(dest - me + n, n)).start()

    def send_tile(step):
        pack_rows(tile_at(step), GROUP, rpd)

    def send_tile_top(step):
        tile = tile_at(step)

        def ext(m):
            before = margin[m, :, lanes_of(tile)].astype(F32)
            after = proj[m, 0:16, lanes_of(tile)].astype(F32)
            return jnp.concatenate((before[mrows - SUB :], after[:SUB]), 0)

        q, dr = features(tile, ext, SUB)
        query[tile, 0:SUB] = q
        drive[tile, 0:SUB] = dr
        pack_rows(tile, 0, GROUP)

    pl.loop(0, early)(send_tile)

    @pl.loop(early, tiles)
    def _(step):
        tile_features(step)
        send_tile(step)

    @pl.when(me > 0)
    def _():
        m_copy.wait_recv()

    @pl.when(me == 0)
    def _():
        margin[...] = jnp.zeros_like(margin)

    pl.loop(0, tiles, unroll=2)(send_tile_top)

    def offset(step):
        return lax.rem(n // 2 + step, n - 1) + 1

    def follow(k, lo, hi):
        if k + 1 < chunks:

            @pl.loop(lo, hi)
            def _(step):
                send_drive(k, offset(step)).wait_send()
                send_drive(k + 1, offset(step)).start()

    loads[1].wait()
    seg = LANES // p
    row_id = lax.broadcasted_iota(jnp.int32, (2 * LANES, 2 * LANES), 0)
    col_id = lax.broadcasted_iota(jnp.int32, (2 * LANES, 2 * LANES), 1)
    inside = lax.rem(row_id, LANES)
    source = LANES + p * lax.rem(inside, seg) + inside // seg - jnp.where(row_id < LANES, 0, p)
    apart = (col_id == source).astype(F32).astype(BF16)
    filt[:, 0:LANES] = jnp.zeros((filt.shape[0], LANES), BF16)

    @pl.loop(0, total // seg, unroll=4)
    def _(t):
        piece = filt[:, pl.ds(pl.multiple_of(t * LANES, LANES), 2 * LANES)]
        wide = jnp.concatenate([piece[k * lc : (k + 1) * lc] for k in range(chunks) for _ in range(p)], 0)
        turned = lax.dot_general(apart, wide, (((1,), (1,)), ((), ())), preferred_element_type=F32)
        at = pl.ds(pl.multiple_of(t * seg, GROUP), seg)
        for k in range(chunks):
            for b in range(p):
                now = turned[b * seg : (b + 1) * seg, k * LANES : (k + 1) * LANES]
                old = turned[LANES + b * seg : LANES + (b + 1) * seg, k * LANES : (k + 1) * LANES]
                tok[k, b, at, :] = jnp.where(lane < b, old, now).astype(BF16)

    for c in loads[2:]:
        c.wait()

    def group_rows(g, a=0):
        return pl.ds(pl.multiple_of(a * n2 + GROUP * g, GROUP), GROUP)

    def filter_spectrum(k):
        follow(k, 0, n // 2)

        @pl.loop(0, groups, unroll=2)
        def _(g):
            wide = jnp.concatenate(
                [
                    jnp.concatenate([tok[k, b, group_rows(g, a), :] for a in range(half)], 0)
                    for b in range(p)
                ],
                1,
            )
            res = jnp.dot(first[g], wide, preferred_element_type=F32)
            wide_f[:, :, group_rows(g), :] = res.astype(BF16).reshape(half, 2, GROUP, p * LANES)

        follow(k, n // 2, n - 1)

        def one(s, which):
            x = wide_f[s].reshape(2 * n2, p * LANES)
            z = jnp.dot(mid[which], x, preferred_element_type=F32)
            spec_f[s] = z.reshape(2, n2, p * LANES)

        one(0, 0)

        @pl.loop(1, half, unroll=5)
        def _(s):
            one(s, 1)

    def slabs(k, ss, which):
        x = jnp.concatenate([spec[s].reshape(2 * n2, LANES) for s in ss], 1)
        z = jnp.dot(mid[which], x, preferred_element_type=F32)
        ys = []
        for j, s in enumerate(ss):
            zr = z[:n2, j * LANES : (j + 1) * LANES]
            zi = z[n2:, j * LANES : (j + 1) * LANES]
            rr = ii = cross = None
            for b in range(p):
                xr = zr if b == 0 else pltpu.roll(zr, b * lc, 1)
                xi = zi if b == 0 else pltpu.roll(zi, b * lc, 1)
                gr = spec_f[s, 0, :, b * LANES : (b + 1) * LANES]
                gi = spec_f[s, 1, :, b * LANES : (b + 1) * LANES]
                add = lambda t, v: v if t is None else t + v
                rr = add(rr, xr * gr)
                ii = add(ii, xi * gi)
                cross = add(cross, xr * gi + xi * gr)
            if which == 0:
                top = lax.broadcasted_iota(jnp.int32, (n2, LANES), 0) == 0
                yr = jnp.where(top, rr, rr - ii)
                yi = jnp.where(top, ii, cross)
            else:
                yr, yi = rr - ii, cross
            ys.append(jnp.concatenate((yr, yi), 0).astype(BF16))
        v = jnp.dot(back[which], jnp.concatenate(ys, 1), preferred_element_type=F32)
        for j, s in enumerate(ss):
            spec[s] = v[:, j * LANES : (j + 1) * LANES].astype(BF16).reshape(2, n2, LANES)

    def convolve(k):
        @pl.loop(1, n)
        def _(i):
            send_drive(k, i).wait_recv()
            if k == 0:
                send_top(i).wait_recv()

        @pl.loop(0, groups, unroll=groups)
        def _(g):
            x = jnp.concatenate([recv[k, group_rows(g, a), :] for a in range(half)], 0)
            res = jnp.dot(first[g], x, preferred_element_type=F32)
            spec[:, :, group_rows(g), :] = res.astype(BF16).reshape(half, 2, GROUP, LANES)

        slabs(k, [0], 0)
        slabs(k, [1], 1)

        @pl.loop(1, half // 2, unroll=half // 2 - 1)
        def _(t):
            slabs(k, [2 * t, 2 * t + 1], 1)

        direct = jnp.concatenate([skip[:, k * lc : (k + 1) * lc]] * p, 1)

        @pl.loop(0, groups, unroll=groups)
        def _(g):
            v = spec[:, :, group_rows(g), :].reshape(2 * half * GROUP, LANES)
            y = jnp.dot(last[g], v, preferred_element_type=F32)
            for a in range(half):
                at = group_rows(g, a)
                both = y[a * GROUP : (a + 1) * GROUP] + direct * recv[k, at, :].astype(F32)
                done[k, at, :] = both.astype(BF16)

        ret[k, me] = done[k, block_rows(me), :]

        @pl.loop(0, n - 1)
        def _(step):
            send_long(k, offset(step)).start()

    for k in range(chunks):
        filter_spectrum(k)
        convolve(k)

    @pl.when(me < n - 1)
    def _():
        m_copy.wait_send()

    @pl.loop(1, n)
    def _(i):
        send_drive(chunks - 1, i).wait_send()
        send_top(i).wait_send()

    @pl.loop(0, tiles)
    def _(step):
        tile = lax.rem(me // own + tiles // 2 + tiles - step, tiles)
        for d in range(own):
            src = tile * own + d

            @pl.when(src != me)
            def _():
                for k in range(chunks):
                    send_long(k, lax.rem(me - src + n, n)).wait_recv()

        parts = [ret[d % chunks, tile * own + d // chunks].astype(F32) for d in range(p)]
        for h in range(p):
            block = None
            for d in range(p):
                shift = ((d - h) % p) * lc
                moved = parts[d] if shift == 0 else pltpu.roll(parts[d], shift, 1)
                block = moved if block is None else jnp.where(lane == d, moved, block)
            drive[tile, pl.ds(h, rpd, stride=p), :] = block
        out[:, lanes_of(tile)] = (query[tile] * drive[tile]).astype(BF16)

    for k in range(chunks):

        @pl.loop(1, n)
        def _(i):
            send_long(k, i).wait_send()


def body(n, projected, taps, filters, skip):
    rows, _, chans = projected.shape
    lc, length = filters.shape
    chunks, sc, p = plan(chans, lc, n)
    rpd = rows // p
    total = length // p
    n1, n2 = factors(2 * total)
    half = n1 // 2
    tables = [jnp.asarray(t) for t in dft_tables(2 * total)]
    vmem = pl.BlockSpec(memory_space=pltpu.VMEM)
    hbm = pl.BlockSpec(memory_space=pl.ANY)
    sems = pltpu.SemaphoreType.DMA((chunks, n))
    blocks = pltpu.VMEM((chunks, n, rpd, LANES), BF16)
    flat = pltpu.VMEM((chunks, total, LANES), BF16)
    moved = jnp.transpose(projected, (1, 0, 2))
    return pl.pallas_call(
        functools.partial(kernel, n, chunks),
        out_shape=jax.ShapeDtypeStruct((rows, chans), BF16),
        in_specs=[hbm, vmem, hbm, vmem] + [hbm] * 4,
        out_specs=vmem,
        scratch_shapes=[
            pltpu.VMEM(moved.shape, BF16),
            pltpu.VMEM((filters.shape[0], LANES + length), BF16),
            *[pltpu.VMEM(t.shape, BF16) for t in tables],
            pltpu.VMEM((3, 16, chans), BF16),
            pltpu.VMEM((chans // LANES, rows, LANES), F32),
            pltpu.VMEM((chans // LANES, rows, LANES), F32),
            blocks,
            pltpu.VMEM((n, GROUP, LANES), BF16),
            flat,
            pltpu.VMEM((chunks, p, total, LANES), BF16),
            pltpu.VMEM((half, 2, n2, p * LANES), BF16),
            pltpu.VMEM((half, 2, n2, p * LANES), F32),
            pltpu.VMEM((half, 2, n2, LANES), BF16),
            flat,
            blocks,
            pltpu.SemaphoreType.DMA((6,)),
            pltpu.SemaphoreType.DMA,
            pltpu.SemaphoreType.DMA,
            sems, sems, sems, sems,
            pltpu.SemaphoreType.DMA((n,)),
            pltpu.SemaphoreType.DMA((n,)),
        ],
        compiler_params=pltpu.CompilerParams(
            collective_id=0, has_side_effects=True, vmem_limit_bytes=56 * 1024 * 1024
        ),
    )(moved, taps, filters, skip.reshape(1, lc), *tables)


def solution(mesh):
    placed = (P(("grp", "seq"), None, None), P(), P("seq", None), P("seq"))
    return jax.shard_map(
        functools.partial(body, mesh.shape["seq"]),
        mesh=mesh, in_specs=placed, out_specs=P(("grp", "seq"), None), check_vma=False,
    )
```

```python
import functools
import math

import jax
import jax.numpy as jnp
import numpy as np
from jax import lax
from jax.experimental import pallas as pl
from jax.experimental.pallas import tpu as pltpu
from jax.sharding import PartitionSpec as P

LANES = 128
SUB = 8
GROUP = 16
MAX_PHASES = 4
F32 = jnp.float32
BF16 = jnp.bfloat16


def factors(order):
    inner = 1 << ((int(math.log2(order)) + 1) // 2)
    return order // inner, inner


def dft_tables(order):
    n1, n2 = factors(order)
    half, hb = n1 // 2, n2 // 2
    groups = n2 // GROUP
    s = np.arange(half)[:, None, None]
    a = np.arange(half)[None, :, None]
    b = np.arange(n2)[None, None, :]
    theta = 2 * np.pi * ((s * (a * n2 + b)) % order) / order
    sign = np.broadcast_to((-1.0) ** np.arange(half)[:, None], (half, n2))
    fwd = np.stack((np.cos(theta), -np.sin(theta)), 1)
    fwd[0, 0] = 1.0
    fwd[0, 1] = sign
    inv = np.stack((2 * np.cos(theta), -2 * np.sin(theta)), 1)
    inv[0, 0] = 1.0
    inv[0, 1] = sign
    inv = inv / order
    eye = np.eye(GROUP)
    fwd_g = fwd.reshape(half, 2, half, groups, GROUP)
    first = np.einsum("srage,ef->gsreaf", fwd_g, eye).reshape(groups, 2 * half * GROUP, half * GROUP)
    inv_g = inv.reshape(half, 2, half, groups, GROUP)
    last = np.einsum("srage,ef->gaesrf", inv_g, eye).reshape(groups, half * GROUP, 2 * half * GROUP)
    k = np.arange(n2)
    phi = 2 * np.pi * (np.outer(k, k) % n2) / n2
    c, d = np.cos(phi), np.sin(phi)
    mid = np.block([[c, d], [-d, c]])
    back = np.block([[c, -d], [d, c]])
    kh = np.arange(hb)
    low = 2 * np.pi * (np.outer(kh, k) % n2) / n2
    odd = 2 * np.pi * (np.outer(half + n1 * kh, k) % order) / order
    mid0 = np.zeros((2 * n2, 2 * n2))
    mid0[:hb, :n2] = np.cos(low)
    mid0[hb:n2, n2:] = np.cos(odd)
    mid0[n2 : n2 + hb, :n2] = -np.sin(low)
    mid0[n2, :n2] = (-1.0) ** k
    mid0[n2 + hb :, n2:] = -np.sin(odd)
    back0 = 2 * mid0.T
    back0[:, 0] /= 2
    back0[:, n2] /= 2
    cast = lambda x: np.ascontiguousarray(x.astype(BF16))
    return cast(first), cast(np.stack((mid0, mid))), cast(np.stack((back0, back))), cast(last)


def plan(chans, lc, n):
    chunks = max(1, MAX_PHASES * lc // LANES)
    lc = lc // chunks
    return chunks, lc, LANES // lc


def kernel(
    n, chunks,
    proj_hbm, taps, filt_hbm, skip, first_hbm, mid_hbm, back_hbm, last_hbm,
    out,
    proj, filt, first, mid, back, last,
    margin, query, drive, pack, recv, tok, wide_f, spec_f, spec, done, ret,
    load, m_send, m_recv, send1, recv1, send2, recv2,
):
    me = lax.axis_index("seq")
    _, rows, chans = proj.shape
    count = taps.shape[0]
    lc = chans // n // chunks
    p = LANES // lc
    rpd = rows // p
    total = rpd * n
    n1, n2 = factors(2 * total)
    half = n1 // 2
    groups = n2 // GROUP
    tiles = chans // LANES
    own = p // chunks
    mrows = margin.shape[1]
    lane = lax.broadcasted_iota(jnp.int32, (1, LANES), 1) // lc

    loads = [
        pltpu.make_async_copy(a, b, load.at[k])
        for k, (a, b) in enumerate(
            ((proj_hbm, proj), (filt_hbm, filt.at[:, pl.ds(LANES, total * p)]), (first_hbm, first), (mid_hbm, mid), (back_hbm, back), (last_hbm, last))
        )
    ]
    for c in loads:
        c.start()

    barrier = pltpu.get_barrier_semaphore()

    @pl.loop(1, n)
    def _(i):
        pl.semaphore_signal(barrier, inc=1, device_id={"seq": lax.rem(me + i, n)})

    def lanes_of(tile):
        return pl.ds(pl.multiple_of(tile * LANES, LANES), LANES)

    def features(tile, ext, many):
        feats = []
        for m in range(3):
            x = ext(m)
            from_row = x.shape[0] - many
            acc = None
            for o in range(count):
                term = taps[o, m : m + 1, lanes_of(tile)] * x[from_row - o : from_row - o + many]
                acc = term if acc is None else acc + term
            feats.append(acc)
        return feats[0], (feats[1] * feats[2]).astype(BF16).astype(F32)

    def tile_at(step):
        return lax.rem(me // own + tiles // 2 + step, tiles)

    def tile_features(step):
        tile = tile_at(step)
        zero = jnp.zeros((SUB, LANES), F32)
        q, d = features(
            tile, lambda m: jnp.concatenate((zero, proj[m, :, lanes_of(tile)].astype(F32)), 0), rows
        )
        query[tile] = q
        drive[tile] = d

    loads[0].wait()
    pl.loop(0, tiles // 2)(tile_features)

    pl.semaphore_wait(barrier, n - 1)
    m_copy = pltpu.make_async_remote_copy(
        src_ref=proj.at[:, pl.ds(rows - mrows, mrows)],
        dst_ref=margin,
        send_sem=m_send,
        recv_sem=m_recv,
        device_id={"seq": lax.rem(me + 1, n)},
    )

    @pl.when(me < n - 1)
    def _():
        m_copy.start()

    early = 3 * tiles // 4
    pl.loop(tiles // 2, early)(tile_features)

    @pl.when(me > 0)
    def _():
        m_copy.wait_recv()

    @pl.when(me == 0)
    def _():
        margin[...] = jnp.zeros_like(margin)

    def block_rows(j):
        return pl.ds(pl.multiple_of(j * rpd, GROUP), rpd)

    def send_drive(k, i):
        dest = lax.rem(me + i, n)
        return pltpu.make_async_remote_copy(
            src_ref=pack.at[k, dest],
            dst_ref=recv.at[k, block_rows(me)],
            send_sem=send1.at[k, i],
            recv_sem=recv1.at[k, i],
            device_id={"seq": dest},
        )

    def send_long(k, i):
        dest = lax.rem(me + i, n)
        return pltpu.make_async_remote_copy(
            src_ref=done.at[k, block_rows(dest)],
            dst_ref=ret.at[k, me],
            send_sem=send2.at[k, i],
            recv_sem=recv2.at[k, i],
            device_id={"seq": dest},
        )

    def send_tile(step):
        tile = tile_at(step)

        def ext(m):
            before = margin[m, :, lanes_of(tile)].astype(F32)
            after = proj[m, 0:16, lanes_of(tile)].astype(F32)
            return jnp.concatenate((before[mrows - SUB :], after[:SUB]), 0)

        q, dr = features(tile, ext, SUB)
        query[tile, 0:SUB] = q
        drive[tile, 0:SUB] = dr
        parts = [drive[tile, pl.ds(h, rpd, stride=p), :] for h in range(p)]
        for d in range(p):
            block = None
            for h in range(p):
                shift = ((h - d) % p) * lc
                moved = parts[h] if shift == 0 else pltpu.roll(parts[h], shift, 1)
                block = moved if block is None else jnp.where(lane == h, moved, block)
            block = block.astype(BF16)
            dest, k = tile * own + d // chunks, d % chunks

            @pl.when(dest == me)
            def _():
                recv[k, block_rows(me), :] = block

            @pl.when(dest != me)
            def _():
                pack[k, dest] = block
                if k == 0:
                    send_drive(k, lax.rem(dest - me + n, n)).start()

    pl.loop(0, early, unroll=2)(send_tile)

    @pl.loop(early, tiles)
    def _(step):
        tile_features(step)
        send_tile(step)

    def offset(step):
        return lax.rem(n // 2 + step, n - 1) + 1

    for k in range(1, chunks):

        @pl.loop(0, n - 1)
        def _(step):
            send_drive(k, offset(step)).start()

    loads[1].wait()
    seg = LANES // p
    row_id = lax.broadcasted_iota(jnp.int32, (2 * LANES, 2 * LANES), 0)
    col_id = lax.broadcasted_iota(jnp.int32, (2 * LANES, 2 * LANES), 1)
    inside = lax.rem(row_id, LANES)
    source = LANES + p * lax.rem(inside, seg) + inside // seg - jnp.where(row_id < LANES, 0, p)
    apart = (col_id == source).astype(F32).astype(BF16)
    filt[:, 0:LANES] = jnp.zeros((filt.shape[0], LANES), BF16)

    @pl.loop(0, total // seg, unroll=4)
    def _(t):
        piece = filt[:, pl.ds(pl.multiple_of(t * LANES, LANES), 2 * LANES)]
        wide = jnp.concatenate([piece[k * lc : (k + 1) * lc] for k in range(chunks) for _ in range(p)], 0)
        turned = lax.dot_general(apart, wide, (((1,), (1,)), ((), ())), preferred_element_type=F32)
        at = pl.ds(pl.multiple_of(t * seg, GROUP), seg)
        for k in range(chunks):
            for b in range(p):
                now = turned[b * seg : (b + 1) * seg, k * LANES : (k + 1) * LANES]
                old = turned[LANES + b * seg : LANES + (b + 1) * seg, k * LANES : (k + 1) * LANES]
                tok[k, b, at, :] = jnp.where(lane < b, old, now).astype(BF16)

    for c in loads[2:]:
        c.wait()

    def group_rows(g, a=0):
        return pl.ds(pl.multiple_of(a * n2 + GROUP * g, GROUP), GROUP)

    def filter_first(k):
        @pl.loop(0, groups, unroll=2)
        def _(g):
            wide = jnp.concatenate(
                [
                    jnp.concatenate([tok[k, b, group_rows(g, a), :] for a in range(half)], 0)
                    for b in range(p)
                ],
                1,
            )
            res = jnp.dot(first[g], wide, preferred_element_type=F32)
            wide_f[:, :, group_rows(g), :] = res.astype(BF16).reshape(half, 2, GROUP, p * LANES)

    def filter_last(k):
        def one(s, which):
            x = wide_f[s].reshape(2 * n2, p * LANES)
            z = jnp.dot(mid[which], x, preferred_element_type=F32)
            spec_f[s] = z.reshape(2, n2, p * LANES)

        one(0, 0)

        @pl.loop(1, half, unroll=5)
        def _(s):
            one(s, 1)

    def slabs(k, ss, which):
        x = jnp.concatenate([spec[s].reshape(2 * n2, LANES) for s in ss], 1)
        z = jnp.dot(mid[which], x, preferred_element_type=F32)
        ys = []
        for j, s in enumerate(ss):
            zr = z[:n2, j * LANES : (j + 1) * LANES]
            zi = z[n2:, j * LANES : (j + 1) * LANES]
            rr = ii = cross = None
            for b in range(p):
                xr = zr if b == 0 else pltpu.roll(zr, b * lc, 1)
                xi = zi if b == 0 else pltpu.roll(zi, b * lc, 1)
                gr = spec_f[s, 0, :, b * LANES : (b + 1) * LANES]
                gi = spec_f[s, 1, :, b * LANES : (b + 1) * LANES]
                add = lambda t, v: v if t is None else t + v
                rr = add(rr, xr * gr)
                ii = add(ii, xi * gi)
                cross = add(cross, xr * gi + xi * gr)
            if which == 0:
                top = lax.broadcasted_iota(jnp.int32, (n2, LANES), 0) == 0
                yr = jnp.where(top, rr, rr - ii)
                yi = jnp.where(top, ii, cross)
            else:
                yr, yi = rr - ii, cross
            ys.append(jnp.concatenate((yr, yi), 0).astype(BF16))
        v = jnp.dot(back[which], jnp.concatenate(ys, 1), preferred_element_type=F32)
        for j, s in enumerate(ss):
            spec[s] = v[:, j * LANES : (j + 1) * LANES].astype(BF16).reshape(2, n2, LANES)

    def convolve(k):
        @pl.loop(1, n)
        def _(i):
            send_drive(k, i).wait_recv()

        @pl.loop(0, groups, unroll=groups)
        def _(g):
            x = jnp.concatenate([recv[k, group_rows(g, a), :] for a in range(half)], 0)
            res = jnp.dot(first[g], x, preferred_element_type=F32)
            spec[:, :, group_rows(g), :] = res.astype(BF16).reshape(half, 2, GROUP, LANES)

        slabs(k, [0], 0)
        slabs(k, [1], 1)

        @pl.loop(1, half // 2, unroll=half // 2 - 1)
        def _(t):
            slabs(k, [2 * t, 2 * t + 1], 1)

        direct = jnp.concatenate([skip[:, k * lc : (k + 1) * lc]] * p, 1)

        @pl.loop(0, groups, unroll=groups)
        def _(g):
            v = spec[:, :, group_rows(g), :].reshape(2 * half * GROUP, LANES)
            y = jnp.dot(last[g], v, preferred_element_type=F32)
            for a in range(half):
                at = group_rows(g, a)
                both = y[a * GROUP : (a + 1) * GROUP] + direct * recv[k, at, :].astype(F32)
                done[k, at, :] = both.astype(BF16)

        ret[k, me] = done[k, block_rows(me), :]

        @pl.loop(0, n - 1)
        def _(step):
            send_long(k, offset(step)).start()

    filter_first(0)
    for k in range(chunks):
        filter_last(k)
        if k + 1 < chunks:
            filter_first(k + 1)
        convolve(k)

    @pl.when(me < n - 1)
    def _():
        m_copy.wait_send()

    for k in range(chunks):

        @pl.loop(1, n)
        def _(i):
            send_drive(k, i).wait_send()

    @pl.loop(0, tiles)
    def _(step):
        tile = lax.rem(me // own + tiles // 2 + tiles - step, tiles)
        for d in range(own):
            src = tile * own + d

            @pl.when(src != me)
            def _():
                for k in range(chunks):
                    send_long(k, lax.rem(me - src + n, n)).wait_recv()

        parts = [ret[d % chunks, tile * own + d // chunks].astype(F32) for d in range(p)]
        for h in range(p):
            block = None
            for d in range(p):
                shift = ((d - h) % p) * lc
                moved = parts[d] if shift == 0 else pltpu.roll(parts[d], shift, 1)
                block = moved if block is None else jnp.where(lane == d, moved, block)
            drive[tile, pl.ds(h, rpd, stride=p), :] = block
        out[:, lanes_of(tile)] = (query[tile] * drive[tile]).astype(BF16)

    for k in range(chunks):

        @pl.loop(1, n)
        def _(i):
            send_long(k, i).wait_send()


def body(n, projected, taps, filters, skip):
    rows, _, chans = projected.shape
    lc, length = filters.shape
    chunks, sc, p = plan(chans, lc, n)
    rpd = rows // p
    total = length // p
    n1, n2 = factors(2 * total)
    half = n1 // 2
    tables = [jnp.asarray(t) for t in dft_tables(2 * total)]
    vmem = pl.BlockSpec(memory_space=pltpu.VMEM)
    hbm = pl.BlockSpec(memory_space=pl.ANY)
    sems = pltpu.SemaphoreType.DMA((chunks, n))
    blocks = pltpu.VMEM((chunks, n, rpd, LANES), BF16)
    flat = pltpu.VMEM((chunks, total, LANES), BF16)
    moved = jnp.transpose(projected, (1, 0, 2))
    return pl.pallas_call(
        functools.partial(kernel, n, chunks),
        out_shape=jax.ShapeDtypeStruct((rows, chans), BF16),
        in_specs=[hbm, vmem, hbm, vmem] + [hbm] * 4,
        out_specs=vmem,
        scratch_shapes=[
            pltpu.VMEM(moved.shape, BF16),
            pltpu.VMEM((filters.shape[0], LANES + length), BF16),
            *[pltpu.VMEM(t.shape, BF16) for t in tables],
            pltpu.VMEM((3, 16, chans), BF16),
            pltpu.VMEM((chans // LANES, rows, LANES), F32),
            pltpu.VMEM((chans // LANES, rows, LANES), F32),
            blocks,
            flat,
            pltpu.VMEM((chunks, p, total, LANES), BF16),
            pltpu.VMEM((half, 2, n2, p * LANES), BF16),
            pltpu.VMEM((half, 2, n2, p * LANES), F32),
            pltpu.VMEM((half, 2, n2, LANES), BF16),
            flat,
            blocks,
            pltpu.SemaphoreType.DMA((6,)),
            pltpu.SemaphoreType.DMA,
            pltpu.SemaphoreType.DMA,
            sems, sems, sems, sems,
        ],
        compiler_params=pltpu.CompilerParams(
            collective_id=0, has_side_effects=True, vmem_limit_bytes=56 * 1024 * 1024
        ),
    )(moved, taps, filters, skip.reshape(1, lc), *tables)


def solution(mesh):
    placed = (P(("grp", "seq"), None, None), P(), P("seq", None), P("seq"))
    return jax.shard_map(
        functools.partial(body, mesh.shape["seq"]),
        mesh=mesh, in_specs=placed, out_specs=P(("grp", "seq"), None), check_vma=False,
    )
```

```python
import functools
import math

import jax
import jax.numpy as jnp
import numpy as np
from jax import lax
from jax.experimental import pallas as pl
from jax.experimental.pallas import tpu as pltpu
from jax.sharding import PartitionSpec as P

LANES = 128
SUB = 8
GROUP = 16
MAX_PHASES = 2
F32 = jnp.float32
BF16 = jnp.bfloat16


def factors(order):
    inner = 1 << ((int(math.log2(order)) + 1) // 2)
    return order // inner, inner


def dft_tables(order):
    n1, n2 = factors(order)
    half, hb = n1 // 2, n2 // 2
    groups = n2 // GROUP
    s = np.arange(half)[:, None, None]
    a = np.arange(half)[None, :, None]
    b = np.arange(n2)[None, None, :]
    theta = 2 * np.pi * ((s * (a * n2 + b)) % order) / order
    sign = np.broadcast_to((-1.0) ** np.arange(half)[:, None], (half, n2))
    fwd = np.stack((np.cos(theta), -np.sin(theta)), 1)
    fwd[0, 0] = 1.0
    fwd[0, 1] = sign
    inv = np.stack((2 * np.cos(theta), -2 * np.sin(theta)), 1)
    inv[0, 0] = 1.0
    inv[0, 1] = sign
    inv = inv / order
    eye = np.eye(GROUP)
    fwd_g = fwd.reshape(half, 2, half, groups, GROUP)
    first = np.einsum("srage,ef->gsreaf", fwd_g, eye).reshape(groups, 2 * half * GROUP, half * GROUP)
    inv_g = inv.reshape(half, 2, half, groups, GROUP)
    last = np.einsum("srage,ef->gaesrf", inv_g, eye).reshape(groups, half * GROUP, 2 * half * GROUP)
    k = np.arange(n2)
    phi = 2 * np.pi * (np.outer(k, k) % n2) / n2
    c, d = np.cos(phi), np.sin(phi)
    mid = np.block([[c, d], [-d, c]])
    back = np.block([[c, -d], [d, c]])
    kh = np.arange(hb)
    low = 2 * np.pi * (np.outer(kh, k) % n2) / n2
    odd = 2 * np.pi * (np.outer(half + n1 * kh, k) % order) / order
    mid0 = np.zeros((2 * n2, 2 * n2))
    mid0[:hb, :n2] = np.cos(low)
    mid0[hb:n2, n2:] = np.cos(odd)
    mid0[n2 : n2 + hb, :n2] = -np.sin(low)
    mid0[n2, :n2] = (-1.0) ** k
    mid0[n2 + hb :, n2:] = -np.sin(odd)
    back0 = 2 * mid0.T
    back0[:, 0] /= 2
    back0[:, n2] /= 2
    cast = lambda x: np.ascontiguousarray(x.astype(BF16))
    return cast(first), cast(np.stack((mid0, mid))), cast(np.stack((back0, back))), cast(last)


def plan(chans, lc, n):
    chunks = max(1, MAX_PHASES * lc // LANES)
    lc = lc // chunks
    return chunks, lc, LANES // lc


def kernel(
    n, chunks,
    proj_hbm, taps, filt_hbm, skip, first_hbm, mid_hbm, back_hbm, last_hbm,
    out,
    proj, filt, first, mid, back, last,
    margin, query, drive, pack, recv, tok, wide_f, spec_f, spec, done, ret,
    load, m_send, m_recv, send1, recv1, send2, recv2,
):
    me = lax.axis_index("seq")
    _, rows, chans = proj.shape
    count = taps.shape[0]
    lc = chans // n // chunks
    p = LANES // lc
    rpd = rows // p
    total = rpd * n
    n1, n2 = factors(2 * total)
    half = n1 // 2
    groups = n2 // GROUP
    tiles = chans // LANES
    own = p // chunks
    mrows = margin.shape[1]
    lane = lax.broadcasted_iota(jnp.int32, (1, LANES), 1) // lc

    loads = [
        pltpu.make_async_copy(a, b, load.at[k])
        for k, (a, b) in enumerate(
            ((proj_hbm, proj), (filt_hbm, filt.at[:, pl.ds(LANES, total * p)]), (first_hbm, first), (mid_hbm, mid), (back_hbm, back), (last_hbm, last))
        )
    ]
    for c in loads:
        c.start()

    barrier = pltpu.get_barrier_semaphore()

    @pl.loop(1, n)
    def _(i):
        pl.semaphore_signal(barrier, inc=1, device_id={"seq": lax.rem(me + i, n)})

    def lanes_of(tile):
        return pl.ds(pl.multiple_of(tile * LANES, LANES), LANES)

    def features(tile, ext, many):
        feats = []
        for m in range(3):
            x = ext(m)
            from_row = x.shape[0] - many
            acc = None
            for o in range(count):
                term = taps[o, m : m + 1, lanes_of(tile)] * x[from_row - o : from_row - o + many]
                acc = term if acc is None else acc + term
            feats.append(acc)
        return feats[0], (feats[1] * feats[2]).astype(BF16).astype(F32)

    def tile_at(step):
        return lax.rem(me // own + tiles // 2 + step, tiles)

    def tile_features(step):
        tile = tile_at(step)
        zero = jnp.zeros((SUB, LANES), F32)
        q, d = features(
            tile, lambda m: jnp.concatenate((zero, proj[m, :, lanes_of(tile)].astype(F32)), 0), rows
        )
        query[tile] = q
        drive[tile] = d

    loads[0].wait()
    pl.loop(0, tiles // 2)(tile_features)

    pl.semaphore_wait(barrier, n - 1)
    m_copy = pltpu.make_async_remote_copy(
        src_ref=proj.at[:, pl.ds(rows - mrows, mrows)],
        dst_ref=margin,
        send_sem=m_send,
        recv_sem=m_recv,
        device_id={"seq": lax.rem(me + 1, n)},
    )

    @pl.when(me < n - 1)
    def _():
        m_copy.start()

    early = 3 * tiles // 4
    pl.loop(tiles // 2, early)(tile_features)

    @pl.when(me > 0)
    def _():
        m_copy.wait_recv()

    @pl.when(me == 0)
    def _():
        margin[...] = jnp.zeros_like(margin)

    def block_rows(j):
        return pl.ds(pl.multiple_of(j * rpd, GROUP), rpd)

    def send_drive(k, i):
        dest = lax.rem(me + i, n)
        return pltpu.make_async_remote_copy(
            src_ref=pack.at[k, dest],
            dst_ref=recv.at[k, block_rows(me)],
            send_sem=send1.at[k, i],
            recv_sem=recv1.at[k, i],
            device_id={"seq": dest},
        )

    def send_long(k, i):
        dest = lax.rem(me + i, n)
        return pltpu.make_async_remote_copy(
            src_ref=done.at[k, block_rows(dest)],
            dst_ref=ret.at[k, me],
            send_sem=send2.at[k, i],
            recv_sem=recv2.at[k, i],
            device_id={"seq": dest},
        )

    def send_tile(step):
        tile = tile_at(step)

        def ext(m):
            before = margin[m, :, lanes_of(tile)].astype(F32)
            after = proj[m, 0:16, lanes_of(tile)].astype(F32)
            return jnp.concatenate((before[mrows - SUB :], after[:SUB]), 0)

        q, dr = features(tile, ext, SUB)
        query[tile, 0:SUB] = q
        drive[tile, 0:SUB] = dr
        parts = [drive[tile, pl.ds(h, rpd, stride=p), :] for h in range(p)]
        for d in range(p):
            block = None
            for h in range(p):
                shift = ((h - d) % p) * lc
                moved = parts[h] if shift == 0 else pltpu.roll(parts[h], shift, 1)
                block = moved if block is None else jnp.where(lane == h, moved, block)
            block = block.astype(BF16)
            dest, k = tile * own + d // chunks, d % chunks

            @pl.when(dest == me)
            def _():
                recv[k, block_rows(me), :] = block

            @pl.when(dest != me)
            def _():
                pack[k, dest] = block
                if k == 0:
                    send_drive(k, lax.rem(dest - me + n, n)).start()

    pl.loop(0, early, unroll=2)(send_tile)

    @pl.loop(early, tiles)
    def _(step):
        tile_features(step)
        send_tile(step)

    def offset(step):
        return lax.rem(n // 2 + step, n - 1) + 1

    def follow(k, lo, hi):
        if k + 1 < chunks:

            @pl.loop(lo, hi)
            def _(step):
                send_drive(k, offset(step)).wait_send()
                send_drive(k + 1, offset(step)).start()

    loads[1].wait()
    seg = LANES // p
    row_id = lax.broadcasted_iota(jnp.int32, (2 * LANES, 2 * LANES), 0)
    col_id = lax.broadcasted_iota(jnp.int32, (2 * LANES, 2 * LANES), 1)
    inside = lax.rem(row_id, LANES)
    source = LANES + p * lax.rem(inside, seg) + inside // seg - jnp.where(row_id < LANES, 0, p)
    apart = (col_id == source).astype(F32).astype(BF16)
    filt[:, 0:LANES] = jnp.zeros((filt.shape[0], LANES), BF16)

    @pl.loop(0, total // seg, unroll=4)
    def _(t):
        piece = filt[:, pl.ds(pl.multiple_of(t * LANES, LANES), 2 * LANES)]
        wide = jnp.concatenate([piece[k * lc : (k + 1) * lc] for k in range(chunks) for _ in range(p)], 0)
        turned = lax.dot_general(apart, wide, (((1,), (1,)), ((), ())), preferred_element_type=F32)
        at = pl.ds(pl.multiple_of(t * seg, GROUP), seg)
        for k in range(chunks):
            for b in range(p):
                now = turned[b * seg : (b + 1) * seg, k * LANES : (k + 1) * LANES]
                old = turned[LANES + b * seg : LANES + (b + 1) * seg, k * LANES : (k + 1) * LANES]
                tok[k, b, at, :] = jnp.where(lane < b, old, now).astype(BF16)

    for c in loads[2:]:
        c.wait()

    def group_rows(g, a=0):
        return pl.ds(pl.multiple_of(a * n2 + GROUP * g, GROUP), GROUP)

    def filter_spectrum(k):
        follow(k, 0, n // 2)

        @pl.loop(0, groups, unroll=2)
        def _(g):
            wide = jnp.concatenate(
                [
                    jnp.concatenate([tok[k, b, group_rows(g, a), :] for a in range(half)], 0)
                    for b in range(p)
                ],
                1,
            )
            res = jnp.dot(first[g], wide, preferred_element_type=F32)
            wide_f[:, :, group_rows(g), :] = res.astype(BF16).reshape(half, 2, GROUP, p * LANES)

        follow(k, n // 2, n - 1)

        def one(s, which):
            x = wide_f[s].reshape(2 * n2, p * LANES)
            z = jnp.dot(mid[which], x, preferred_element_type=F32)
            spec_f[s] = z.reshape(2, n2, p * LANES)

        one(0, 0)

        @pl.loop(1, half, unroll=5)
        def _(s):
            one(s, 1)

    def slabs(k, ss, which):
        x = jnp.concatenate([spec[s].reshape(2 * n2, LANES) for s in ss], 1)
        z = jnp.dot(mid[which], x, preferred_element_type=F32)
        ys = []
        for j, s in enumerate(ss):
            zr = z[:n2, j * LANES : (j + 1) * LANES]
            zi = z[n2:, j * LANES : (j + 1) * LANES]
            rr = ii = cross = None
            for b in range(p):
                xr = zr if b == 0 else pltpu.roll(zr, b * lc, 1)
                xi = zi if b == 0 else pltpu.roll(zi, b * lc, 1)
                gr = spec_f[s, 0, :, b * LANES : (b + 1) * LANES]
                gi = spec_f[s, 1, :, b * LANES : (b + 1) * LANES]
                add = lambda t, v: v if t is None else t + v
                rr = add(rr, xr * gr)
                ii = add(ii, xi * gi)
                cross = add(cross, xr * gi + xi * gr)
            if which == 0:
                top = lax.broadcasted_iota(jnp.int32, (n2, LANES), 0) == 0
                yr = jnp.where(top, rr, rr - ii)
                yi = jnp.where(top, ii, cross)
            else:
                yr, yi = rr - ii, cross
            ys.append(jnp.concatenate((yr, yi), 0).astype(BF16))
        v = jnp.dot(back[which], jnp.concatenate(ys, 1), preferred_element_type=F32)
        for j, s in enumerate(ss):
            spec[s] = v[:, j * LANES : (j + 1) * LANES].astype(BF16).reshape(2, n2, LANES)

    def convolve(k):
        @pl.loop(1, n)
        def _(i):
            send_drive(k, i).wait_recv()

        @pl.loop(0, groups, unroll=groups)
        def _(g):
            x = jnp.concatenate([recv[k, group_rows(g, a), :] for a in range(half)], 0)
            res = jnp.dot(first[g], x, preferred_element_type=F32)
            spec[:, :, group_rows(g), :] = res.astype(BF16).reshape(half, 2, GROUP, LANES)

        slabs(k, [0], 0)
        slabs(k, [1], 1)

        @pl.loop(1, half // 2, unroll=half // 2 - 1)
        def _(t):
            slabs(k, [2 * t, 2 * t + 1], 1)

        direct = jnp.concatenate([skip[:, k * lc : (k + 1) * lc]] * p, 1)

        @pl.loop(0, groups, unroll=groups)
        def _(g):
            v = spec[:, :, group_rows(g), :].reshape(2 * half * GROUP, LANES)
            y = jnp.dot(last[g], v, preferred_element_type=F32)
            for a in range(half):
                at = group_rows(g, a)
                both = y[a * GROUP : (a + 1) * GROUP] + direct * recv[k, at, :].astype(F32)
                done[k, at, :] = both.astype(BF16)

        ret[k, me] = done[k, block_rows(me), :]

        @pl.loop(0, n - 1)
        def _(step):
            send_long(k, offset(step)).start()

    for k in range(chunks):
        filter_spectrum(k)
        convolve(k)

    @pl.when(me < n - 1)
    def _():
        m_copy.wait_send()

    @pl.loop(1, n)
    def _(i):
        send_drive(chunks - 1, i).wait_send()

    @pl.loop(0, tiles)
    def _(step):
        tile = lax.rem(me // own + tiles // 2 + tiles - step, tiles)
        for d in range(own):
            src = tile * own + d

            @pl.when(src != me)
            def _():
                for k in range(chunks):
                    send_long(k, lax.rem(me - src + n, n)).wait_recv()

        parts = [ret[d % chunks, tile * own + d // chunks].astype(F32) for d in range(p)]
        for h in range(p):
            block = None
            for d in range(p):
                shift = ((d - h) % p) * lc
                moved = parts[d] if shift == 0 else pltpu.roll(parts[d], shift, 1)
                block = moved if block is None else jnp.where(lane == d, moved, block)
            drive[tile, pl.ds(h, rpd, stride=p), :] = block
        out[:, lanes_of(tile)] = (query[tile] * drive[tile]).astype(BF16)

    for k in range(chunks):

        @pl.loop(1, n)
        def _(i):
            send_long(k, i).wait_send()


def body(n, projected, taps, filters, skip):
    rows, _, chans = projected.shape
    lc, length = filters.shape
    chunks, sc, p = plan(chans, lc, n)
    rpd = rows // p
    total = length // p
    n1, n2 = factors(2 * total)
    half = n1 // 2
    tables = [jnp.asarray(t) for t in dft_tables(2 * total)]
    vmem = pl.BlockSpec(memory_space=pltpu.VMEM)
    hbm = pl.BlockSpec(memory_space=pl.ANY)
    sems = pltpu.SemaphoreType.DMA((chunks, n))
    blocks = pltpu.VMEM((chunks, n, rpd, LANES), BF16)
    flat = pltpu.VMEM((chunks, total, LANES), BF16)
    moved = jnp.transpose(projected, (1, 0, 2))
    return pl.pallas_call(
        functools.partial(kernel, n, chunks),
        out_shape=jax.ShapeDtypeStruct((rows, chans), BF16),
        in_specs=[hbm, vmem, hbm, vmem] + [hbm] * 4,
        out_specs=vmem,
        scratch_shapes=[
            pltpu.VMEM(moved.shape, BF16),
            pltpu.VMEM((filters.shape[0], LANES + length), BF16),
            *[pltpu.VMEM(t.shape, BF16) for t in tables],
            pltpu.VMEM((3, 16, chans), BF16),
            pltpu.VMEM((chans // LANES, rows, LANES), F32),
            pltpu.VMEM((chans // LANES, rows, LANES), F32),
            blocks,
            flat,
            pltpu.VMEM((chunks, p, total, LANES), BF16),
            pltpu.VMEM((half, 2, n2, p * LANES), BF16),
            pltpu.VMEM((half, 2, n2, p * LANES), F32),
            pltpu.VMEM((half, 2, n2, LANES), BF16),
            flat,
            blocks,
            pltpu.SemaphoreType.DMA((6,)),
            pltpu.SemaphoreType.DMA,
            pltpu.SemaphoreType.DMA,
            sems, sems, sems, sems,
        ],
        compiler_params=pltpu.CompilerParams(
            collective_id=0, has_side_effects=True, vmem_limit_bytes=56 * 1024 * 1024
        ),
    )(moved, taps, filters, skip.reshape(1, lc), *tables)


def solution(mesh):
    placed = (P(("grp", "seq"), None, None), P(), P("seq", None), P("seq"))
    return jax.shard_map(
        functools.partial(body, mesh.shape["seq"]),
        mesh=mesh, in_specs=placed, out_specs=P(("grp", "seq"), None), check_vma=False,
    )
```
